128 devices in a mesh: pipe: 2 (over x_hi), ctx: 8 (over x_lo, z), tp: 8 (over y, core).
Axes of the slice: x: 4 (x_hi: 2, x_lo: 2; x = x_hi * 2 + x_lo), y: 4, z: 4, core: 2. Of those that a mesh axis runs over, the one named last changes fastest.
Arguments:
- queries: bfloat16 [2, 2, 4096, 8192], P('pipe', None, 'ctx', 'tp'), may hold values from -220 to 220
- keys: bfloat16 [2, 2, 4096, 1024], P('pipe', None, 'ctx', 'tp'), may hold values from -8 to 8
- values: bfloat16 [2, 2, 4096, 1024], P('pipe', None, 'ctx', 'tp'), may hold values from -16 to 16
- doc_start: int32 [2, 4096], P(None, 'ctx'), may hold values from 0 to 4095, as said below
- owners: int32 [2, 128], P(None, 'ctx'), may hold values from 0 to 7, as said below
Outputs:
- balanced: bfloat16 [2, 2, 8, 8, 3, 32, 8192], P('pipe', None, 'ctx', None, None, None, 'tp')
The draws below stay inside these ranges and needn't reach their ends.
Inputs may be any that keep to these rules, and one draw needn't show every extreme that they name: doc_start[m, i] is the first token of token i's document: it never decreases along the slab, is at most i, i - doc_start[m, i] < 256, and every slab holds a document of exactly 256 tokens. `owners`: of the 16 tracts that lie on one index of ctx, at most 3 have the same owner, and in every such block some owner gets exactly 3.
All inputs are finite; a program needn't handle non-finite values.
Results may differ from the reference program's by a relative error of at most 0.0063.
Values may be sent and summed in bfloat16 or wider, within the bound.
A program may use at most 128 MiB of HBM per device.

```python
import math
import jax
import jax.numpy as jnp
from jax import lax

QUERY_HEADS = 64
KEY_VALUE_HEADS = 8
HEAD_WIDTH = 128
MICRO_BATCHES = 2
TRACTS_DEV = 16
RELAY_SECTIONS = 2
SLAB_TOKENS = 4096
CH = 32
DOCMAX = 256
NCHUNK = 128
CAP = 3
N_CTX = 8


def drawn_pair(key):
    starting_keys = 1.2 * jnp.clip(jax.random.normal(jax.random.fold_in(key, 11), (RELAY_SECTIONS, MICRO_BATCHES, SLAB_TOKENS, KEY_VALUE_HEADS * HEAD_WIDTH), jnp.float32), -5.0, 5.0)
    base_queries = 1.2 * jnp.clip(jax.random.normal(jax.random.fold_in(key, 12), (RELAY_SECTIONS, MICRO_BATCHES, SLAB_TOKENS, QUERY_HEADS * HEAD_WIDTH), jnp.float32), -5.0, 5.0)
    return (base_queries, starting_keys)


def draw_queries(key, part):
    return drawn_pair(key)[0].astype(jnp.bfloat16)


def draw_keys(key, part):
    return drawn_pair(key)[1].astype(jnp.bfloat16)


def start_list(key):
    lengths = jax.random.randint(key, (SLAB_TOKENS,), 1, DOCMAX + 1)
    long_doc = jax.random.randint(jax.random.fold_in(key, 1), (), 0, 4)
    lengths = jnp.where(jnp.arange(SLAB_TOKENS) == long_doc, DOCMAX, lengths)
    doc_ends = jnp.minimum(jnp.cumsum(lengths), SLAB_TOKENS)
    boundary = jnp.zeros((SLAB_TOKENS + 1,), jnp.int32).at[doc_ends].set(1)
    row_ids = jnp.arange(SLAB_TOKENS, dtype=jnp.int32)
    return lax.cummax(jnp.where(boundary[:SLAB_TOKENS] == 1, row_ids, 0), axis=0)


def draw_doc_start(key, part):
    keys_all = jax.random.split(key, MICRO_BATCHES)
    return jax.vmap(start_list)(keys_all).astype(jnp.int32)


def owner_block(key):
    owner_count = NCHUNK // TRACTS_DEV
    base_count = TRACTS_DEV // owner_count
    shuffle = jax.random.permutation(jax.random.fold_in(key, 1), owner_count)
    second_move = jax.random.randint(jax.random.fold_in(key, 2), (), 0, 2)
    owner_ids = jnp.arange(owner_count)
    counts = base_count + (owner_ids == shuffle[0]).astype(jnp.int32) - (owner_ids == shuffle[1]).astype(jnp.int32)
    counts = counts + second_move * ((owner_ids == shuffle[2]).astype(jnp.int32) - (owner_ids == shuffle[3]).astype(jnp.int32))
    bounds_at = jnp.cumsum(counts)
    slot_ids = jnp.arange(TRACTS_DEV)
    listing = jnp.sum((bounds_at[None, :] <= slot_ids[:, None]).astype(jnp.int32), axis=1)
    return jax.random.permutation(jax.random.fold_in(key, 3), listing)


def draw_owners(key, part):
    owner_count = NCHUNK // TRACTS_DEV
    keys_all = jax.random.split(key, MICRO_BATCHES * owner_count)
    blocks = jax.vmap(owner_block)(keys_all)
    return blocks.reshape(MICRO_BATCHES, NCHUNK).astype(jnp.int32)


def shard_levels(key, dims, pieces, least, high):
    factor_of = 1.0
    for position, blocks in pieces:
        heights = jax.random.uniform(jax.random.fold_in(jax.random.fold_in(key, 6), position), (blocks,), jnp.float32, least / len(pieces), high / len(pieces))
        factor_of = factor_of * jnp.repeat(jnp.exp(heights), dims[position] // blocks).reshape((-1,) + (1,) * (len(dims) - 1 - position))
    return factor_of


def noise(key, extent, spread, limit, pieces=(), kind=jnp.bfloat16):
    entries = jax.random.normal(key, extent, jnp.float32) * spread
    if len(pieces) > 0:
        entries = shard_levels(key, extent, pieces, -0.22, 0.18) * entries
    return jnp.clip(entries, min=-limit, max=limit).astype(kind)


def setup_inputs(seed: int = 0) -> dict:
    arg_keys = jax.random.split(jax.random.key(seed), 6)
    queries = draw_queries(jax.random.fold_in(arg_keys[5], 71), 0)
    keys = draw_keys(jax.random.fold_in(arg_keys[5], 71), 0)
    values = noise(arg_keys[2], (RELAY_SECTIONS, MICRO_BATCHES, SLAB_TOKENS, KEY_VALUE_HEADS * HEAD_WIDTH), 4.0, 16.0, ((0, 2), (2, 8), (3, 8)))
    doc_start = draw_doc_start(jax.random.fold_in(arg_keys[5], 71), 0)
    owners = draw_owners(jax.random.fold_in(arg_keys[5], 71), 0)
    return dict(queries=queries, keys=keys, values=values, doc_start=doc_start, owners=owners)


def attend_tract(query_rows, key_win, value_win, first_key, row_ids, row_starts):
    tract_rows = query_rows.shape[0]
    key_span = key_win.shape[0]
    kv_heads = key_win.shape[1] // HEAD_WIDTH
    query_group_width = query_rows.shape[1] // (kv_heads * HEAD_WIDTH)
    heads_for_query = query_rows.reshape(tract_rows, kv_heads, query_group_width, HEAD_WIDTH).astype(jnp.float32)
    heads_for_key = key_win.reshape(key_span, kv_heads, HEAD_WIDTH).astype(jnp.float32)
    value_heads = value_win.reshape(key_span, kv_heads, HEAD_WIDTH).astype(jnp.float32)
    scores = jnp.einsum('tkgd,jkd->tkgj', heads_for_query, heads_for_key) / math.sqrt(HEAD_WIDTH)
    key_ids = first_key + jnp.arange(key_span, dtype=jnp.int32)
    allowed = (key_ids[None, :] >= row_starts[:, None]) & (key_ids[None, :] <= row_ids[:, None])
    scores = jnp.where(allowed[:, None, None, :], scores, -1e+30)
    row_max = lax.optimization_barrier(jnp.max(scores, axis=-1, keepdims=True))
    exp_terms = jnp.exp(scores - row_max)
    denom_sum = lax.optimization_barrier(jnp.sum(exp_terms, axis=-1))
    weights = lax.optimization_barrier(exp_terms.astype(jnp.bfloat16)).astype(jnp.float32)
    attended = jnp.einsum('tkgj,jkd->tkgd', weights, value_heads) / denom_sum[..., None]
    return attended.reshape(tract_rows, -1).astype(jnp.bfloat16)

def section_rows(section_in, key_rows, value_rows, starts):
    window = DOCMAX + CH
    local_ids = jnp.arange(CH, dtype=jnp.int32)

    def per_tract(tract_id):
        first_row = (tract_id * CH).astype(jnp.int32)
        win_start = jnp.clip(first_row + CH - window, 0, SLAB_TOKENS - window).astype(jnp.int32)
        tract_in = lax.dynamic_slice_in_dim(section_in, first_row, CH, 0)
        key_win = lax.dynamic_slice_in_dim(key_rows, win_start, window, 0)
        value_win = lax.dynamic_slice_in_dim(value_rows, win_start, window, 0)
        row_starts = lax.dynamic_slice_in_dim(starts, first_row, CH, 0)
        return attend_tract(tract_in, key_win, value_win, win_start, first_row + local_ids, row_starts)
    answers = lax.map(per_tract, jnp.arange(NCHUNK, dtype=jnp.int32))
    return answers.reshape(SLAB_TOKENS, -1)

def to_owner(rows_done, owner_list):
    blocks = owner_list.reshape(N_CTX, TRACTS_DEV)
    positions = jnp.arange(TRACTS_DEV, dtype=jnp.int32)
    earlier = positions[None, :] < positions[:, None]
    same_owner = blocks[:, :, None] == blocks[:, None, :]
    rank_of = lax.optimization_barrier(jnp.sum(same_owner & earlier[None], axis=2)).astype(jnp.int32).reshape(-1)
    source = jnp.repeat(jnp.arange(N_CTX, dtype=jnp.int32), TRACTS_DEV)
    tract_block = rows_done.reshape(NCHUNK, CH, rows_done.shape[-1])
    zero_buf = jnp.zeros((N_CTX, N_CTX, CAP, CH, rows_done.shape[-1]), jnp.bfloat16)
    return zero_buf.at[owner_list, source, rank_of].set(tract_block)

def reference(queries, keys, values, doc_start, owners):
    section_outputs = []
    previous = []
    for section_index in range(RELAY_SECTIONS):
        layer_rows = []
        owner_blocks = []
        for micro_index in range(MICRO_BATCHES):
            section_in = queries[section_index, micro_index]
            if section_index > 0:
                section_in = (section_in.astype(jnp.float32) + previous[micro_index].astype(jnp.float32)).astype(jnp.bfloat16)
            rows_done = section_rows(section_in, keys[section_index, micro_index], values[section_index, micro_index], doc_start[micro_index])
            layer_rows.append(rows_done)
            owner_blocks.append(to_owner(rows_done, owners[micro_index]))
        previous = layer_rows
        section_outputs.append(jnp.stack(owner_blocks))
    return jnp.stack(section_outputs)
```

```python
import functools
import math

import jax
import jax.numpy as jnp
from jax import lax
from jax.experimental import pallas as pl
from jax.experimental.pallas import tpu as pltpu
from jax.sharding import PartitionSpec as P

HEAD_WIDTH = 128
TRACTS_DEV = 16
CH = 32
CAP = 3
DOCMAX = 256
BLOCK = 128
SPAN = BLOCK + DOCMAX
Z = 4
MESH = pl.DeviceIdType.MESH
MASKED = -1e30


def kernel(
    q_hbm,
    k_hbm,
    v_hbm,
    starts_ref,
    owners_ref,
    out_ref,
    q_buf,
    c_buf,
    a_buf,
    b_buf,
    s_buf,
    k_win,
    v_win,
    bias,
    pick,
    dest,
    q_sem,
    kv_sem,
    halo_send,
    halo_recv,
    dest_sem,
    ex_send,
    ex_recv,
    fw_send,
    fw_recv,
    z_send,
    z_recv,
    own_sem,
):
    pipe = lax.axis_index("pipe")
    ctx = lax.axis_index("ctx")
    ctx_count = lax.axis_size("ctx")
    x_lo = ctx // Z
    z = lax.rem(ctx, Z)
    units, rows, width = q_buf.shape
    micro = k_win.shape[0]
    per_micro = units // micro
    scale = 1.0 / math.sqrt(HEAD_WIDTH)

    beside = {"ctx": (1 - x_lo) * Z + z}
    across = {"pipe": 1 - pipe, "ctx": (1 - x_lo) * Z + z}
    right = {"ctx": lax.rem(ctx + 1, ctx_count)}

    def q_load(u):
        m, g = u // per_micro, lax.rem(u, per_micro)
        return pltpu.make_async_copy(
            q_hbm.at[0, m, :, pl.ds(pl.multiple_of(g * width, width), width)],
            q_buf.at[u],
            q_sem.at[u],
        )

    def kv_load(m, which):
        src, dst = ((k_hbm, k_win), (v_hbm, v_win))[which]
        return pltpu.make_async_copy(
            src.at[0, m], dst.at[m, pl.ds(DOCMAX, rows)], kv_sem.at[m, which]
        )

    def halo(m, which):
        src, dst = ((k_hbm, k_win), (v_hbm, v_win))[which]
        return pltpu.make_async_remote_copy(
            src_ref=src.at[0, m, pl.ds(rows - DOCMAX, DOCMAX)],
            dst_ref=dst.at[m, pl.ds(0, DOCMAX)],
            send_sem=halo_send.at[m, which],
            recv_sem=halo_recv.at[m, which],
            device_id=right,
            device_id_type=MESH,
        )

    def dest_copy():
        return pltpu.make_async_remote_copy(
            src_ref=dest.at[0],
            dst_ref=dest.at[1],
            send_sem=dest_sem.at[0],
            recv_sem=dest_sem.at[1],
            device_id=beside,
            device_id_type=MESH,
        )

    def exchange(u):
        return pltpu.make_async_remote_copy(
            src_ref=a_buf.at[u],
            dst_ref=b_buf.at[u],
            send_sem=ex_send.at[u],
            recv_sem=ex_recv.at[u],
            device_id=beside,
            device_id_type=MESH,
        )

    def forward(u):
        return pltpu.make_async_remote_copy(
            src_ref=b_buf.at[u],
            dst_ref=c_buf.at[u],
            send_sem=fw_send.at[u],
            recv_sem=fw_recv.at[u],
            device_id=across,
            device_id_type=MESH,
        )

    def out_slice(u, z_source):
        m, g = u // per_micro, lax.rem(u, per_micro)
        return out_ref.at[
            m, :, z_source, :, :, pl.ds(pl.multiple_of(g * width, width), width)
        ]

    def spread(u, z_to, z_from):
        return pltpu.make_async_remote_copy(
            src_ref=s_buf.at[u, :, z_to],
            dst_ref=out_slice(u, z_from),
            send_sem=z_send.at[u, z_to],
            recv_sem=z_recv.at[u, z_from],
            device_id={"ctx": x_lo * Z + z_to},
            device_id_type=MESH,
        )

    def keep(u):
        return pltpu.make_async_copy(
            s_buf.at[u, :, z], out_slice(u, z), own_sem.at[u]
        )

    for m in range(micro):
        for which in range(2):
            kv_load(m, which).start()

    @pl.loop(0, units)
    def _(u):
        q_load(u).start()

    barrier = pltpu.get_barrier_semaphore()
    for step in range(1, 2 * Z):
        pl.semaphore_signal(
            barrier,
            inc=1,
            device_id={"ctx": lax.rem(ctx + step, 2 * Z)},
            device_id_type=MESH,
        )
    pl.semaphore_signal(barrier, inc=1, device_id=across, device_id_type=MESH)
    pl.semaphore_wait(barrier, 2 * Z)

    for m in range(micro):
        for which in range(2):
            halo(m, which).start()

    lane = lax.broadcasted_iota(jnp.int32, (8, rows), 1)
    sub = lax.broadcasted_iota(jnp.int32, (8, rows), 0)
    tract = lax.shift_right_logical(lane, 5)
    slot = jnp.zeros((8, rows), jnp.int32)
    for m in range(micro):
        names = [owners_ref[m, t] for t in range(TRACTS_DEV)]
        for t in range(TRACTS_DEV):
            rank = jnp.int32(0)
            for earlier in range(t):
                rank = rank + jnp.where(names[earlier] == names[t], 1, 0)
            here = (tract == t) & (sub == m)
            slot = jnp.where(here, names[t] * CAP + rank, slot)
    dest[0] = slot * CH + (lane & (CH - 1))
    dest_copy().start()

    row_at = lax.broadcasted_iota(jnp.int32, (BLOCK, BLOCK), 0)
    col_at = lax.broadcasted_iota(jnp.int32, (BLOCK, BLOCK), 1)
    for m in range(micro):
        for b in range(rows // BLOCK):
            line = starts_ref[pl.ds(m, 1), pl.ds(b * BLOCK, BLOCK)].astype(jnp.float32)
            column = jnp.transpose(jnp.broadcast_to(line, (BLOCK, BLOCK))).astype(jnp.int32)
            first = column - (ctx * rows + b * BLOCK - DOCMAX)
            for part in range(SPAN // BLOCK):
                key_at = col_at + part * BLOCK
                allowed = (key_at >= first) & (key_at <= row_at + DOCMAX)
                bias[m, pl.ds(b * BLOCK, BLOCK), pl.ds(part * BLOCK, BLOCK)] = jnp.where(
                    allowed, 0.0, MASKED
                )

    def pick_rows(m, whose):
        target = dest[whose, pl.ds(m, 1), :] - x_lo * (Z * CAP * CH)
        slots = Z * CAP * CH
        wanted = lax.broadcasted_iota(jnp.int32, (slots, rows), 0)
        pick[m, whose] = jnp.where(wanted == target, 1.0, 0.0).astype(jnp.bfloat16)

    for m in range(micro):
        pick_rows(m, 0)
    dest_copy().wait()
    for m in range(micro):
        pick_rows(m, 1)

    def produce(u):
        m = u // per_micro
        q_load(u).wait()

        @pl.when(lax.rem(u, per_micro) == 0)
        def _():
            for which in range(2):
                kv_load(m, which).wait()
                halo(m, which).wait()

        @pl.when(pipe == 1)
        def _():
            forward(u).wait_recv()
            q_buf[u] = (
                q_buf[u].astype(jnp.float32) + c_buf[u].astype(jnp.float32)
            ).astype(jnp.bfloat16)

        for b in range(rows // BLOCK):
            keys = k_win[m, pl.ds(b * BLOCK, SPAN), :]
            vals = v_win[m, pl.ds(b * BLOCK, SPAN), :]
            for h in range(width // HEAD_WIDTH):
                q = q_buf[u, pl.ds(b * BLOCK, BLOCK), pl.ds(h * HEAD_WIDTH, HEAD_WIDTH)]
                scores = lax.dot_general(
                    q, keys, (((1,), (1,)), ((), ())), preferred_element_type=jnp.float32
                )
                scores = scores + bias[m, pl.ds(b * BLOCK, BLOCK), :]
                top = jnp.max(scores, axis=1, keepdims=True)
                terms = jnp.exp((scores - top) * scale)
                denom = jnp.sum(terms, axis=1, keepdims=True)
                mixed = jnp.dot(
                    terms.astype(jnp.bfloat16), vals, preferred_element_type=jnp.float32
                )
                a_buf[u, pl.ds(b * BLOCK, BLOCK), pl.ds(h * HEAD_WIDTH, HEAD_WIDTH)] = (
                    mixed / denom
                ).astype(jnp.bfloat16)
        exchange(u).start()

    def consume(u):
        m = u // per_micro
        exchange(u).wait_recv()

        @pl.when(pipe == 0)
        def _():
            forward(u).start()

        for whose, source in ((0, a_buf), (1, b_buf)):
            picked = jnp.dot(pick[m, whose], source[u], preferred_element_type=jnp.float32)
            place = x_lo if whose == 0 else 1 - x_lo
            s_buf[u, place] = picked.astype(jnp.bfloat16).reshape(Z, CAP, CH, width)
        for step in (2, 1, 3):
            spread(u, lax.rem(z + step, Z), z).start()
        keep(u).start()

    @pl.loop(0, units + 1)
    def _(step):
        @pl.when(step < units)
        def _():
            produce(step)

        @pl.when(step >= 1)
        def _():
            consume(step - 1)

    @pl.loop(0, units)
    def _(u):
        exchange(u).wait_send()

        @pl.when(pipe == 0)
        def _():
            forward(u).wait_send()

        keep(u).wait()
        for step in range(1, Z):
            other = lax.rem(z + step, Z)
            spread(u, other, z).wait_send()
            spread(u, z, other).wait_recv()


def local(queries, keys, values, doc_start, owners):
    _, micro, rows, width_q = queries.shape
    unit_width = HEAD_WIDTH
    units = micro * (width_q // unit_width)
    bf16, f32, i32 = jnp.bfloat16, jnp.float32, jnp.int32
    dma = pltpu.SemaphoreType.DMA
    anywhere = pl.BlockSpec(memory_space=pl.ANY)
    out = pl.pallas_call(
        kernel,
        out_shape=jax.ShapeDtypeStruct((micro, 2, Z, CAP, CH, width_q), bf16),
        in_specs=[
            anywhere,
            anywhere,
            anywhere,
            pl.BlockSpec(memory_space=pltpu.VMEM),
            pl.BlockSpec(memory_space=pltpu.SMEM),
        ],
        out_specs=anywhere,
        scratch_shapes=[
            pltpu.VMEM((units, rows, unit_width), bf16),
            pltpu.VMEM((units, rows, unit_width), bf16),
            pltpu.VMEM((units, rows, unit_width), bf16),
            pltpu.VMEM((units, rows, unit_width), bf16),
            pltpu.VMEM((units, 2, Z, CAP, CH, unit_width), bf16),
            pltpu.VMEM((micro, DOCMAX + rows, HEAD_WIDTH), bf16),
            pltpu.VMEM((micro, DOCMAX + rows, HEAD_WIDTH), bf16),
            pltpu.VMEM((micro, rows, SPAN), f32),
            pltpu.VMEM((micro, 2, Z * CAP * CH, rows), bf16),
            pltpu.VMEM((2, 8, rows), i32),
            dma((units,)),
            dma((micro, 2)),
            dma((micro, 2)),
            dma((micro, 2)),
            dma((2,)),
            dma((units,)),
            dma((units,)),
            dma((units,)),
            dma((units,)),
            dma((units, Z)),
            dma((units, Z)),
            dma((units,)),
        ],
        compiler_params=pltpu.CompilerParams(
            collective_id=0, has_side_effects=True, vmem_limit_bytes=48 * 1024 * 1024
        ),
    )(queries, keys, values, doc_start, owners)
    return out.reshape(1, micro, 1, 2 * Z, CAP, CH, width_q)


def solution(mesh):
    return jax.shard_map(
        local,
        mesh=mesh,
        in_specs=(
            P("pipe", None, "ctx", "tp"),
            P("pipe", None, "ctx", "tp"),
            P("pipe", None, "ctx", "tp"),
            P(None, "ctx"),
            P(None, "ctx"),
        ),
        out_specs=P("pipe", None, "ctx", None, None, None, "tp"),
        check_vma=False,
    )
```

```python
import functools
import math

import jax
import jax.numpy as jnp
from jax import lax
from jax.experimental import pallas as pl
from jax.experimental.pallas import tpu as pltpu
from jax.sharding import PartitionSpec as P

HEAD_WIDTH = 128
TRACTS_DEV = 16
CH = 32
CAP = 3
DOCMAX = 256
BLOCK = 128
SPAN = BLOCK + DOCMAX
CHUNK = 256
LAG = 6
Z = 4
MESH = pl.DeviceIdType.MESH
MASKED = -1e30


def kernel(
    q_hbm,
    k_hbm,
    v_hbm,
    starts_hbm,
    owners_hbm,
    out_ref,
    q_buf,
    c_buf,
    a_buf,
    b_buf,
    s_buf,
    k_win,
    v_win,
    bias,
    pick,
    dest,
    starts_ref,
    owners_ref,
    small_sem,
    q_sem,
    kv_sem,
    halo_send,
    halo_recv,
    dest_sem,
    ex_send,
    ex_recv,
    fw_send,
    fw_recv,
    to_send,
    to_recv,
    own_sem,
):
    pipe = lax.axis_index("pipe")
    ctx = lax.axis_index("ctx")
    ctx_count = lax.axis_size("ctx")
    x_lo = ctx // Z
    z = lax.rem(ctx, Z)
    units, rows, width = q_buf.shape
    micro = k_win.shape[0]
    per_micro = units // micro
    chunks = rows // CHUNK
    half = chunks // 2
    steps = units * chunks
    slots = Z * CAP * CH
    scale = math.log2(math.e) / math.sqrt(HEAD_WIDTH)

    beside = {"ctx": (1 - x_lo) * Z + z}
    across = {"pipe": 1 - pipe, "ctx": (1 - x_lo) * Z + z}
    right = {"ctx": lax.rem(ctx + 1, ctx_count)}

    def chunk_at(step):
        return (
            step
            + jnp.where(step // half == 1, half, 0)
            - jnp.where(step // half == 2, half, 0)
        )

    def first_row(chunk):
        part = lax.rem(lax.rem(chunk, chunks) + half, chunks)
        return pl.multiple_of(part * CHUNK, CHUNK)

    def columns(u):
        return pl.ds(pl.multiple_of(lax.rem(u, per_micro) * width, width), width)

    def q_load(u):
        return pltpu.make_async_copy(
            q_hbm.at[0, u // per_micro, :, columns(u)], q_buf.at[u], q_sem.at[u]
        )

    def starts_load():
        return pltpu.make_async_copy(starts_hbm, starts_ref, small_sem.at[0])

    def owners_load():
        return pltpu.make_async_copy(owners_hbm, owners_ref, small_sem.at[1])

    def kv_load(m, which):
        src, dst = ((k_hbm, k_win), (v_hbm, v_win))[which]
        return pltpu.make_async_copy(
            src.at[0, m], dst.at[m, pl.ds(DOCMAX, rows)], kv_sem.at[m, which]
        )

    def halo(m, which):
        src, dst = ((k_hbm, k_win), (v_hbm, v_win))[which]
        return pltpu.make_async_remote_copy(
            src_ref=src.at[0, m, pl.ds(rows - DOCMAX, DOCMAX)],
            dst_ref=dst.at[m, pl.ds(0, DOCMAX)],
            send_sem=halo_send.at[m, which],
            recv_sem=halo_recv.at[m, which],
            device_id=right,
            device_id_type=MESH,
        )

    def dest_copy():
        return pltpu.make_async_remote_copy(
            src_ref=dest.at[0],
            dst_ref=dest.at[1],
            send_sem=dest_sem.at[0],
            recv_sem=dest_sem.at[1],
            device_id=beside,
            device_id_type=MESH,
        )

    def exchange(chunk):
        u, span = chunk // chunks, pl.ds(first_row(chunk), CHUNK)
        return pltpu.make_async_remote_copy(
            src_ref=a_buf.at[u, span],
            dst_ref=b_buf.at[u, span],
            send_sem=ex_send.at[chunk],
            recv_sem=ex_recv.at[chunk],
            device_id=beside,
            device_id_type=MESH,
        )

    def forward(chunk):
        u, span = chunk // chunks, pl.ds(first_row(chunk), CHUNK)
        return pltpu.make_async_remote_copy(
            src_ref=b_buf.at[u, span],
            dst_ref=c_buf.at[u, span],
            send_sem=fw_send.at[chunk],
            recv_sem=fw_recv.at[chunk],
            device_id=across,
            device_id_type=MESH,
        )

    def spread_near(u, z_to, z_from):
        return pltpu.make_async_remote_copy(
            src_ref=s_buf.at[u, :, z_to],
            dst_ref=out_ref.at[u // per_micro, :, z_from, :, :, columns(u)],
            send_sem=to_send.at[u, z_to],
            recv_sem=to_recv.at[u, z_from],
            device_id={"ctx": x_lo * Z + z_to},
            device_id_type=MESH,
        )

    def keep_near(u):
        return pltpu.make_async_copy(
            s_buf.at[u, :, z],
            out_ref.at[u // per_micro, :, z, :, :, columns(u)],
            own_sem.at[u],
        )

    def spread_far(u, to, source):
        return pltpu.make_async_remote_copy(
            src_ref=s_buf.at[u, to // Z, lax.rem(to, Z)],
            dst_ref=out_ref.at[
                u // per_micro, source // Z, lax.rem(source, Z), :, :, columns(u)
            ],
            send_sem=to_send.at[u, to],
            recv_sem=to_recv.at[u, source],
            device_id={"ctx": to},
            device_id_type=MESH,
        )

    def keep_far(u):
        return pltpu.make_async_copy(
            s_buf.at[u, x_lo, z],
            out_ref.at[u // per_micro, x_lo, z, :, :, columns(u)],
            own_sem.at[u],
        )

    starts_load().start()
    for which in range(2):
        kv_load(0, which).start()
    q_load(0).start()
    q_load(1).start()
    owners_load().start()
    for which in range(2):
        kv_load(1, which).start()

    @pl.loop(2, units)
    def _(u):
        q_load(u).start()

    barrier = pltpu.get_barrier_semaphore()
    for step in range(1, 2 * Z):
        pl.semaphore_signal(
            barrier,
            inc=1,
            device_id={"ctx": lax.rem(ctx + step, 2 * Z)},
            device_id_type=MESH,
        )
    pl.semaphore_signal(barrier, inc=1, device_id=across, device_id_type=MESH)

    def mask_rows(m):
        row_at = lax.broadcasted_iota(jnp.int32, (BLOCK, BLOCK), 0)
        col_at = lax.broadcasted_iota(jnp.int32, (BLOCK, BLOCK), 1)
        for b in range(rows // BLOCK):
            line = starts_ref[pl.ds(m, 1), pl.ds(b * BLOCK, BLOCK)].astype(jnp.float32)
            column = jnp.transpose(jnp.broadcast_to(line, (BLOCK, BLOCK))).astype(jnp.int32)
            first = column - (ctx * rows + b * BLOCK - DOCMAX)
            for part in range(SPAN // BLOCK):
                key_at = col_at + part * BLOCK
                allowed = (key_at >= first) & (key_at <= row_at + DOCMAX)
                bias[m, pl.ds(b * BLOCK, BLOCK), pl.ds(part * BLOCK, BLOCK)] = jnp.where(
                    allowed, 0.0, MASKED
                )

    def find_dest():
        owners_load().wait()
        lane = lax.broadcasted_iota(jnp.int32, (8, rows), 1)
        sub = lax.broadcasted_iota(jnp.int32, (8, rows), 0)
        tract = lax.shift_right_logical(lane, 5)
        slot = jnp.zeros((8, rows), jnp.int32)
        for m in range(micro):
            names = [owners_ref[m, t] for t in range(TRACTS_DEV)]
            for t in range(TRACTS_DEV):
                rank = jnp.int32(0)
                for earlier in range(t):
                    rank = rank + jnp.where(names[earlier] == names[t], 1, 0)
                here = (tract == t) & (sub == m)
                slot = jnp.where(here, names[t] * CAP + rank, slot)
        dest[0] = slot * CH + (lane & (CH - 1))

    def pick_rows(m, whose, at, first, count):
        target = dest[whose, pl.ds(m, 1), :] - first
        wanted = lax.broadcasted_iota(jnp.int32, (count, rows), 0)
        pick[m, pl.ds(at, count), :] = jnp.where(wanted == target, 1.0, 0.0).astype(
            jnp.bfloat16
        )

    def attend(chunk):
        u = chunk // chunks
        m = u // per_micro
        base = first_row(chunk)
        for b in range(CHUNK // BLOCK):
            span = pl.ds(base + b * BLOCK, BLOCK)
            keys = k_win[m, pl.ds(base + b * BLOCK, SPAN), :]
            vals = v_win[m, pl.ds(base + b * BLOCK, SPAN), :]
            scores = lax.dot_general(
                q_buf[u, span, :],
                keys,
                (((1,), (1,)), ((), ())),
                preferred_element_type=jnp.float32,
            )
            scores = scores + bias[m, span, :]
            top = jnp.max(scores, axis=1, keepdims=True)
            terms = jnp.exp2((scores - top) * scale)
            denom = jnp.sum(terms, axis=1, keepdims=True)
            mixed = jnp.dot(
                terms.astype(jnp.bfloat16), vals, preferred_element_type=jnp.float32
            )
            a_buf[u, span, :] = (mixed / denom).astype(jnp.bfloat16)

    def await_inputs(chunk):
        u, part = chunk // chunks, lax.rem(chunk, chunks)
        m, g = u // per_micro, lax.rem(u, per_micro)

        @pl.when(part == 0)
        def _():
            q_load(u).wait()

        @pl.when((part == 0) & (g == 0))
        def _():
            for which in range(2):
                kv_load(m, which).wait()

        @pl.when((part == half) & (g == 0))
        def _():
            for which in range(2):
                halo(m, which).wait_recv()

    starts_load().wait()
    mask_rows(0)
    pl.semaphore_wait(barrier, 2 * Z)
    for which in range(2):
        halo(0, which).start()

    @pl.when(pipe == 0)
    def _():
        @pl.loop(0, steps + LAG)
        def _(step):
            @pl.when(step < steps)
            def _():
                chunk = chunk_at(step)
                await_inputs(chunk)
                attend(chunk)
                exchange(chunk).start()

            @pl.when(step >= LAG)
            def _():
                chunk = chunk_at(step - LAG)
                u = chunk // chunks
                m = u // per_micro
                exchange(chunk).wait_recv()
                forward(chunk).start()

                @pl.when(lax.rem(chunk, chunks) == chunks - 1)
                def _():
                    for place, source, first in (
                        (x_lo, a_buf, 0),
                        (1 - x_lo, b_buf, slots),
                    ):
                        picked = jnp.dot(
                            pick[m, pl.ds(first, slots), :],
                            source[u],
                            preferred_element_type=jnp.float32,
                        )
                        s_buf[u, place] = picked.astype(jnp.bfloat16).reshape(
                            Z, CAP, CH, width
                        )
                    for turn in (2, 1, 3):
                        spread_near(u, lax.rem(z + turn, Z), z).start()
                    keep_near(u).start()

            @pl.when(step == 0)
            def _():
                find_dest()
                dest_copy().start()
                pick_rows(0, 0, 0, x_lo * slots, slots)

            @pl.when(step == half)
            def _():
                dest_copy().wait()
                pick_rows(0, 1, slots, x_lo * slots, slots)

            @pl.when(step == 4 * chunks)
            def _():
                for which in range(2):
                    halo(1, which).start()
                mask_rows(1)

            @pl.when(step == 5 * chunks)
            def _():
                pick_rows(1, 0, 0, x_lo * slots, slots)

            @pl.when(step == 6 * chunks)
            def _():
                pick_rows(1, 1, slots, x_lo * slots, slots)

        @pl.loop(0, steps)
        def _(chunk):
            exchange(chunk).wait_send()
            forward(chunk).wait_send()

        @pl.loop(0, units)
        def _(u):
            keep_near(u).wait()
            for turn in range(1, Z):
                other = lax.rem(z + turn, Z)
                spread_near(u, other, z).wait_send()
                spread_near(u, z, other).wait_recv()

    @pl.when(pipe == 1)
    def _():
        find_dest()
        for m in range(micro):
            pick_rows(m, 0, 0, 0, 2 * slots)
        mask_rows(1)

        @pl.loop(0, steps)
        def _(step):
            chunk = chunk_at(step)
            u = chunk // chunks
            m = u // per_micro
            span = pl.ds(first_row(chunk), CHUNK)
            @pl.when(step == 4 * chunks)
            def _():
                for which in range(2):
                    halo(1, which).start()
            await_inputs(chunk)
            forward(chunk).wait_recv()
            q_buf[u, span, :] = (
                q_buf[u, span, :].astype(jnp.float32) + c_buf[u, span, :].astype(jnp.float32)
            ).astype(jnp.bfloat16)
            attend(chunk)

            @pl.when(lax.rem(chunk, chunks) == chunks - 1)
            def _():
                picked = jnp.dot(pick[m], a_buf[u], preferred_element_type=jnp.float32)
                s_buf[u] = picked.astype(jnp.bfloat16).reshape(2, Z, CAP, CH, width)
                for turn in (6, 2, 5, 7, 4, 1, 3):
                    spread_far(u, lax.rem(ctx + turn, 2 * Z), ctx).start()
                keep_far(u).start()

        @pl.loop(0, units)
        def _(u):
            keep_far(u).wait()
            for turn in range(1, 2 * Z):
                other = lax.rem(ctx + turn, 2 * Z)
                spread_far(u, other, ctx).wait_send()
                spread_far(u, ctx, other).wait_recv()

    for m in range(micro):
        for which in range(2):
            halo(m, which).wait_send()


def local(queries, keys, values, doc_start, owners):
    _, micro, rows, width_q = queries.shape
    unit_width = HEAD_WIDTH
    units = micro * (width_q // unit_width)
    steps = units * (rows // CHUNK)
    bf16, f32, i32 = jnp.bfloat16, jnp.float32, jnp.int32
    dma = pltpu.SemaphoreType.DMA
    in_hbm = pl.BlockSpec(memory_space=pltpu.HBM)
    out = pl.pallas_call(
        kernel,
        out_shape=jax.ShapeDtypeStruct((micro, 2, Z, CAP, CH, width_q), bf16),
        in_specs=[in_hbm] * 5,
        out_specs=pl.BlockSpec(memory_space=pl.ANY),
        scratch_shapes=[
            pltpu.VMEM((units, rows, unit_width), bf16),
            pltpu.VMEM((units, rows, unit_width), bf16),
            pltpu.VMEM((units, rows, unit_width), bf16),
            pltpu.VMEM((units, rows, unit_width), bf16),
            pltpu.VMEM((units, 2, Z, CAP, CH, unit_width), bf16),
            pltpu.VMEM((micro, DOCMAX + rows, HEAD_WIDTH), bf16),
            pltpu.VMEM((micro, DOCMAX + rows, HEAD_WIDTH), bf16),
            pltpu.VMEM((micro, rows, SPAN), f32),
            pltpu.VMEM((micro, 2 * Z * CAP * CH, rows), bf16),
            pltpu.VMEM((2, 8, rows), i32),
            pltpu.VMEM((micro, rows), i32),
            pltpu.SMEM((micro, TRACTS_DEV), i32),
            dma((2,)),
            dma((units,)),
            dma((micro, 2)),
            dma((micro, 2)),
            dma((micro, 2)),
            dma((2,)),
            dma((steps,)),
            dma((steps,)),
            dma((steps,)),
            dma((steps,)),
            dma((units, 2 * Z)),
            dma((units, 2 * Z)),
            dma((units,)),
        ],
        compiler_params=pltpu.CompilerParams(
            collective_id=0, has_side_effects=True, vmem_limit_bytes=48 * 1024 * 1024
        ),
    )(*[pltpu.with_memory_space_constraint(a, pltpu.HBM) for a in (queries, keys, values, doc_start, owners)])
    return out.reshape(1, micro, 1, 2 * Z, CAP, CH, width_q)


def solution(mesh):
    return jax.shard_map(
        local,
        mesh=mesh,
        in_specs=(
            P("pipe", None, "ctx", "tp"),
            P("pipe", None, "ctx", "tp"),
            P("pipe", None, "ctx", "tp"),
            P(None, "ctx"),
            P(None, "ctx"),
        ),
        out_specs=P("pipe", None, "ctx", None, None, None, "tp"),
        check_vma=False,
    )
```

```python
import functools
import math

import jax
import jax.numpy as jnp
from jax import lax
from jax.experimental import pallas as pl
from jax.experimental.pallas import tpu as pltpu
from jax.sharding import PartitionSpec as P

HEAD_WIDTH = 128
TRACTS_DEV = 16
CH = 32
CAP = 3
DOCMAX = 256
BLOCK = 128
SPAN = BLOCK + DOCMAX
CHUNK = 256
EARLY = 7
FIRST = 2
MORE = 4
Z = 4
MESH = pl.DeviceIdType.MESH
MASKED = -1e30


def kernel(
    q_hbm,
    k_hbm,
    v_hbm,
    starts_hbm,
    owners_hbm,
    out_ref,
    q_buf,
    relay,
    c_buf,
    a_buf,
    b_buf,
    s_buf,
    k_win,
    v_win,
    bias,
    pick,
    dest,
    starts_ref,
    owners_ref,
    small_sem,
    q_sem,
    kv_sem,
    halo_send,
    halo_recv,
    relay_sem,
    dest_sem,
    ex_recv,
    fw_recv,
    all_send,
    all_recv,
):
    pipe = lax.axis_index("pipe")
    ctx = lax.axis_index("ctx")
    ctx_count = lax.axis_size("ctx")
    x_lo = ctx // Z
    z = lax.rem(ctx, Z)
    units, rows, width = q_buf.shape
    micro = k_win.shape[0]
    per_micro = units // micro
    chunks = rows // CHUNK
    steps = units * chunks
    slots = Z * CAP * CH
    scale = math.log2(math.e) / math.sqrt(HEAD_WIDTH)

    beside = {"ctx": (1 - x_lo) * Z + z}
    across = {"pipe": 1 - pipe, "ctx": (1 - x_lo) * Z + z}
    right = {"ctx": lax.rem(ctx + 1, ctx_count)}

    def chunk_at(step):
        return jnp.where(
            step < EARLY,
            2 * step,
            jnp.where(step < 2 * EARLY, 2 * (step - EARLY) + 1, step),
        )

    def first_row(chunk):
        return pl.multiple_of((1 - lax.rem(chunk, chunks)) * CHUNK, CHUNK)

    def columns(u):
        return pl.ds(pl.multiple_of(lax.rem(u, per_micro) * width, width), width)

    def q_load(u):
        return pltpu.make_async_copy(
            q_hbm.at[0, u // per_micro, :, columns(u)], q_buf.at[u], q_sem.at[u]
        )

    def starts_load():
        return pltpu.make_async_copy(starts_hbm, starts_ref, small_sem.at[0])

    def owners_load():
        return pltpu.make_async_copy(owners_hbm, owners_ref, small_sem.at[1])

    def kv_load(m, which):
        src, dst = ((k_hbm, k_win), (v_hbm, v_win))[which]
        return pltpu.make_async_copy(
            src.at[0, m],
            dst.at[m, pl.ds(DOCMAX, rows), pl.ds(0, HEAD_WIDTH)],
            kv_sem.at[m, which],
        )

    def halo_ends(m, which):
        src, dst = ((k_hbm, k_win), (v_hbm, v_win))[which]
        return (
            src.at[0, m, pl.ds(rows - DOCMAX, DOCMAX)],
            dst.at[m, pl.ds(0, DOCMAX), pl.ds(0, HEAD_WIDTH)],
        )

    def halo(m, which):
        src, dst = halo_ends(m, which)
        return pltpu.make_async_remote_copy(
            src_ref=src,
            dst_ref=dst,
            send_sem=halo_send.at[m, which],
            recv_sem=halo_recv.at[m, which],
            device_id=right,
            device_id_type=MESH,
        )

    def relay_z(m, which):
        return (2 * m + which + Z - 1) % Z

    def to_relay(m, which):
        return pltpu.make_async_remote_copy(
            src_ref=halo_ends(m, which)[0],
            dst_ref=relay,
            send_sem=halo_send.at[m, which],
            recv_sem=relay_sem.at[0],
            device_id={"ctx": relay_z(m, which)},
            device_id_type=MESH,
        )

    def from_relay(m, which):
        return pltpu.make_async_remote_copy(
            src_ref=relay,
            dst_ref=halo_ends(m, which)[1],
            send_sem=relay_sem.at[1],
            recv_sem=halo_recv.at[m, which],
            device_id={"ctx": Z},
            device_id_type=MESH,
        )

    def send_halo(m):
        for which in range(2):
            via = relay_z(m, which)
            if via == Z - 1:
                direct = ctx < ctx_count - 1
            else:
                direct = (ctx < ctx_count - 1) & (ctx != Z - 1)

                @pl.when(ctx == Z - 1)
                def _():
                    to_relay(m, which).start()

            @pl.when(direct)
            def _():
                halo(m, which).start()

    def pass_halo(m):
        for which in range(2):
            via = relay_z(m, which)
            if via != Z - 1:

                @pl.when(ctx == via)
                def _():
                    to_relay(m, which).wait_recv()
                    from_relay(m, which).start()

    def dest_copy():
        return pltpu.make_async_remote_copy(
            src_ref=dest.at[0],
            dst_ref=dest.at[1],
            send_sem=dest_sem.at[0],
            recv_sem=dest_sem.at[1],
            device_id=beside,
            device_id_type=MESH,
        )

    def exchange(chunk):
        u, span = chunk // chunks, pl.ds(first_row(chunk), CHUNK)
        return pltpu.make_async_remote_copy(
            src_ref=a_buf.at[u, span],
            dst_ref=b_buf.at[u, span],
            send_sem=all_send.at[0],
            recv_sem=ex_recv.at[chunk],
            device_id=beside,
            device_id_type=MESH,
        )

    def forward(chunk):
        u, span = chunk // chunks, pl.ds(first_row(chunk), CHUNK)
        return pltpu.make_async_remote_copy(
            src_ref=b_buf.at[u, span],
            dst_ref=c_buf.at[u, span],
            send_sem=all_send.at[1],
            recv_sem=fw_recv.at[chunk],
            device_id=across,
            device_id_type=MESH,
        )

    def spread_near(u, z_to, z_from):
        return pltpu.make_async_remote_copy(
            src_ref=s_buf.at[u, :, z_to],
            dst_ref=out_ref.at[u // per_micro, :, z_from, :, :, columns(u)],
            send_sem=all_send.at[2],
            recv_sem=all_recv.at[0],
            device_id={"ctx": x_lo * Z + z_to},
            device_id_type=MESH,
        )

    def keep_near(u):
        return pltpu.make_async_copy(
            s_buf.at[u, :, z],
            out_ref.at[u // per_micro, :, z, :, :, columns(u)],
            all_recv.at[0],
        )

    def spread_far(u, to, source):
        return pltpu.make_async_remote_copy(
            src_ref=s_buf.at[u, to // Z, lax.rem(to, Z)],
            dst_ref=out_ref.at[
                u // per_micro, source // Z, lax.rem(source, Z), :, :, columns(u)
            ],
            send_sem=all_send.at[2],
            recv_sem=all_recv.at[0],
            device_id={"ctx": to},
            device_id_type=MESH,
        )

    def keep_far(u):
        return pltpu.make_async_copy(
            s_buf.at[u, x_lo, z],
            out_ref.at[u // per_micro, x_lo, z, :, :, columns(u)],
            all_recv.at[0],
        )

    barrier = pltpu.get_barrier_semaphore()
    for step in range(1, 2 * Z):
        pl.semaphore_signal(
            barrier,
            inc=1,
            device_id={"ctx": lax.rem(ctx + step, 2 * Z)},
            device_id_type=MESH,
        )
    pl.semaphore_signal(barrier, inc=1, device_id=across, device_id_type=MESH)

    starts_load().start()
    for which in range(2):
        kv_load(0, which).start()
    owners_load().start()

    @pl.loop(0, units)
    def _(u):
        q_load(u).start()

    for which in range(2):
        kv_load(1, which).start()

    def mask_rows(m):
        row_at = lax.broadcasted_iota(jnp.int32, (BLOCK, BLOCK), 0)
        col_at = lax.broadcasted_iota(jnp.int32, (BLOCK, BLOCK), 1)
        for b in range(rows // BLOCK):
            line = starts_ref[pl.ds(m, 1), pl.ds(b * BLOCK, BLOCK)].astype(jnp.float32)
            column = jnp.transpose(jnp.broadcast_to(line, (BLOCK, BLOCK))).astype(jnp.int32)
            first = column - (ctx * rows + b * BLOCK - DOCMAX)
            for part in range(SPAN // BLOCK):
                key_at = col_at + part * BLOCK
                allowed = (key_at >= first) & (key_at <= row_at + DOCMAX)
                bias[m, pl.ds(b * BLOCK, BLOCK), pl.ds(part * BLOCK, BLOCK)] = jnp.where(
                    allowed, 0.0, MASKED
                )

    def find_dest():
        owners_load().wait()
        lane = lax.broadcasted_iota(jnp.int32, (8, rows), 1)
        sub = lax.broadcasted_iota(jnp.int32, (8, rows), 0)
        tract = lax.shift_right_logical(lane, 5)
        slot = jnp.zeros((8, rows), jnp.int32)
        for m in range(micro):
            names = [owners_ref[m, t] for t in range(TRACTS_DEV)]
            for t in range(TRACTS_DEV):
                rank = jnp.int32(0)
                for earlier in range(t):
                    rank = rank + jnp.where(names[earlier] == names[t], 1, 0)
                here = (tract == t) & (sub == m)
                slot = jnp.where(here, names[t] * CAP + rank, slot)
        dest[0] = slot * CH + (lane & (CH - 1))

    def pick_rows(m, whose, at, first, count):
        target = dest[whose, pl.ds(m, 1), :] - first
        wanted = lax.broadcasted_iota(jnp.int32, (count, rows), 0)
        pick[m, pl.ds(at, count), :] = jnp.where(wanted == target, 1.0, 0.0).astype(
            jnp.bfloat16
        )

    def attend(chunk, section):
        u = chunk // chunks
        m = u // per_micro
        base = first_row(chunk)
        spans = [pl.ds(base + b * BLOCK, BLOCK) for b in range(CHUNK // BLOCK)]
        windows = [pl.ds(base + b * BLOCK, SPAN) for b in range(CHUNK // BLOCK)]
        terms = []
        for span, window in zip(spans, windows):
            q = q_buf[u, span, :]
            if section:
                q = (q.astype(jnp.float32) + c_buf[u, span, :].astype(jnp.float32)).astype(
                    jnp.bfloat16
                )
            scores = lax.dot_general(
                q, k_win[m, window, :], (((1,), (1,)), ((), ())), preferred_element_type=jnp.float32
            )
            scores = scores + bias[m, span, :]
            top = jnp.max(scores, axis=1, keepdims=True)
            terms.append(jnp.exp2((scores - top) * scale).astype(jnp.bfloat16))
        for span, window, weights in zip(spans, windows, terms):
            mixed = jnp.dot(weights, v_win[m, window, :], preferred_element_type=jnp.float32)
            a_buf[u, span, :] = (mixed[:, :HEAD_WIDTH] / mixed[:, HEAD_WIDTH:]).astype(
                jnp.bfloat16
            )

    def await_inputs(chunk):
        u, part = chunk // chunks, lax.rem(chunk, chunks)
        m, g = u // per_micro, lax.rem(u, per_micro)

        @pl.when(part == 0)
        def _():
            q_load(u).wait()

        @pl.when((part == 0) & (g == 0))
        def _():
            for which in range(2):
                kv_load(m, which).wait()

        @pl.when((part == 1) & (g == 0) & (ctx > 0))
        def _():
            for which in range(2):
                halo(m, which).wait_recv()

    ones = jnp.ones((DOCMAX + rows, HEAD_WIDTH), jnp.bfloat16)
    for m in range(micro):
        v_win[m, :, pl.ds(HEAD_WIDTH, HEAD_WIDTH)] = ones

    @pl.when(ctx == 0)
    def _():
        for m in range(micro):
            for window in (k_win, v_win):
                window[m, pl.ds(0, DOCMAX), pl.ds(0, HEAD_WIDTH)] = jnp.zeros(
                    (DOCMAX, HEAD_WIDTH), jnp.bfloat16
                )

    starts_load().wait()
    mask_rows(0)

    @pl.when(pipe == 0)
    def _():
        def lead(turn):
            return jnp.minimum(FIRST + turn + jnp.minimum(turn, MORE), steps)

        @pl.loop(0, FIRST)
        def _(step):
            chunk = chunk_at(step)
            await_inputs(chunk)
            attend(chunk, 0)

        find_dest()
        pl.semaphore_wait(barrier, 2 * Z)
        dest_copy().start()
        send_halo(0)
        for step in range(FIRST):
            exchange(chunk_at(step)).start()

        @pl.loop(0, steps)
        def _(turn):
            @pl.loop(lead(turn), lead(turn + 1))
            def _(step):
                chunk = chunk_at(step)
                await_inputs(chunk)
                attend(chunk, 0)
                exchange(chunk).start()

            chunk = chunk_at(turn)
            u = chunk // chunks
            m = u // per_micro
            exchange(chunk).wait_recv()
            forward(chunk).start()

            @pl.when(lax.rem(chunk, chunks) == chunks - 1)
            def _():
                for place, source, first in ((x_lo, a_buf, 0), (1 - x_lo, b_buf, slots)):
                    picked = jnp.dot(
                        pick[m, pl.ds(first, slots), :],
                        source[u],
                        preferred_element_type=jnp.float32,
                    )
                    s_buf[u, place] = picked.astype(jnp.bfloat16).reshape(Z, CAP, CH, width)
                for to in (2, 1, 3):
                    spread_near(u, lax.rem(z + to, Z), z).start()
                keep_near(u).start()

            @pl.when(turn == 0)
            def _():
                pass_halo(0)
                dest_copy().wait()
                for whose in range(2):
                    pick_rows(0, whose, whose * slots, x_lo * slots, slots)

            @pl.when(turn == 1)
            def _():
                send_halo(1)
                mask_rows(1)

            @pl.when(turn == 3)
            def _():
                pass_halo(1)
                for whose in range(2):
                    pick_rows(1, whose, whose * slots, x_lo * slots, slots)

        pltpu.make_async_copy(a_buf, a_buf, all_send.at[0]).wait()
        pltpu.make_async_copy(b_buf, b_buf, all_send.at[1]).wait()
        sent = s_buf.at[pl.ds(0, units - units // Z)]
        pltpu.make_async_copy(sent, sent, all_send.at[2]).wait()

    @pl.when(pipe == 1)
    def _():
        find_dest()
        pl.semaphore_wait(barrier, 2 * Z)
        for m in range(micro):
            send_halo(m)
        for m in range(micro):
            pick_rows(m, 0, 0, 0, 2 * slots)
        mask_rows(1)
        for m in range(micro):
            pass_halo(m)

        @pl.loop(0, steps)
        def _(step):
            chunk = chunk_at(step)
            u = chunk // chunks
            m = u // per_micro
            await_inputs(chunk)
            forward(chunk).wait_recv()
            attend(chunk, 1)

            @pl.when(lax.rem(chunk, chunks) == chunks - 1)
            def _():
                picked = jnp.dot(pick[m], a_buf[u], preferred_element_type=jnp.float32)
                s_buf[u] = picked.astype(jnp.bfloat16).reshape(2, Z, CAP, CH, width)
                for turn in (6, 2, 5, 7, 4, 1, 3):
                    spread_far(u, lax.rem(ctx + turn, 2 * Z), ctx).start()
                keep_far(u).start()

        sent = s_buf.at[pl.ds(0, units - units // (2 * Z))]
        pltpu.make_async_copy(sent, sent, all_send.at[2]).wait()

    pltpu.make_async_copy(out_ref, out_ref, all_recv.at[0]).wait()

    @pl.when(ctx < ctx_count - 1)
    def _():
        for m in range(micro):
            for which in range(2):
                halo(m, which).wait_send()

    for m in range(micro):
        for which in range(2):
            if relay_z(m, which) != Z - 1:

                @pl.when(ctx == relay_z(m, which))
                def _():
                    from_relay(m, which).wait_send()


def local(queries, keys, values, doc_start, owners):
    _, micro, rows, width_q = queries.shape
    unit_width = HEAD_WIDTH
    units = micro * (width_q // unit_width)
    steps = units * (rows // CHUNK)
    bf16, f32, i32 = jnp.bfloat16, jnp.float32, jnp.int32
    dma = pltpu.SemaphoreType.DMA
    in_hbm = pl.BlockSpec(memory_space=pltpu.HBM)
    out = pl.pallas_call(
        kernel,
        out_shape=jax.ShapeDtypeStruct((micro, 2, Z, CAP, CH, width_q), bf16),
        in_specs=[in_hbm] * 5,
        out_specs=pl.BlockSpec(memory_space=pl.ANY),
        scratch_shapes=[
            pltpu.VMEM((units, rows, unit_width), bf16),
            pltpu.VMEM((DOCMAX, HEAD_WIDTH), bf16),
            pltpu.VMEM((units, rows, unit_width), bf16),
            pltpu.VMEM((units, rows, unit_width), bf16),
            pltpu.VMEM((units, rows, unit_width), bf16),
            pltpu.VMEM((units, 2, Z, CAP, CH, unit_width), bf16),
            pltpu.VMEM((micro, DOCMAX + rows, HEAD_WIDTH), bf16),
            pltpu.VMEM((micro, DOCMAX + rows, 2 * HEAD_WIDTH), bf16),
            pltpu.VMEM((micro, rows, SPAN), f32),
            pltpu.VMEM((micro, 2 * Z * CAP * CH, rows), bf16),
            pltpu.VMEM((2, 8, rows), i32),
            pltpu.VMEM((micro, rows), i32),
            pltpu.SMEM((micro, TRACTS_DEV), i32),
            dma((2,)),
            dma((units,)),
            dma((micro, 2)),
            dma((micro, 2)),
            dma((micro, 2)),
            dma((2,)),
            dma((2,)),
            dma((steps,)),
            dma((steps,)),
            dma((3,)),
            dma((1,)),
        ],
        compiler_params=pltpu.CompilerParams(
            collective_id=0, has_side_effects=True, vmem_limit_bytes=48 * 1024 * 1024
        ),
    )(*[pltpu.with_memory_space_constraint(a, pltpu.HBM) for a in (queries, keys, values, doc_start, owners)])
    return out.reshape(1, micro, 1, 2 * Z, CAP, CH, width_q)


def solution(mesh):
    return jax.shard_map(
        local,
        mesh=mesh,
        in_specs=(
            P("pipe", None, "ctx", "tp"),
            P("pipe", None, "ctx", "tp"),
            P("pipe", None, "ctx", "tp"),
            P(None, "ctx"),
            P(None, "ctx"),
        ),
        out_specs=P("pipe", None, "ctx", None, None, None, "tp"),
        check_vma=False,
    )
```

```python
import functools
import math

import jax
import jax.numpy as jnp
from jax import lax
from jax.experimental import pallas as pl
from jax.experimental.pallas import tpu as pltpu
from jax.sharding import PartitionSpec as P

HEAD_WIDTH = 128
TRACTS_DEV = 16
CH = 32
CAP = 3
DOCMAX = 256
BLOCK = 128
SPAN = BLOCK + DOCMAX
CHUNK = 256
EARLY = 7
FIRST = 1
MORE = 4
Z = 4
MESH = pl.DeviceIdType.MESH
MASKED = -1e30


def kernel(
    q_hbm,
    k_hbm,
    v_hbm,
    starts_hbm,
    owners_hbm,
    out_ref,
    q_buf,
    relay,
    c_buf,
    a_buf,
    b_buf,
    s_buf,
    k_win,
    v_win,
    bias,
    pick,
    dest,
    starts_ref,
    owners_ref,
    small_sem,
    q_sem,
    kv_sem,
    halo_send,
    halo_recv,
    relay_sem,
    dest_sem,
    ex_recv,
    fw_recv,
    all_send,
    all_recv,
):
    pipe = lax.axis_index("pipe")
    ctx = lax.axis_index("ctx")
    ctx_count = lax.axis_size("ctx")
    x_lo = ctx // Z
    z = lax.rem(ctx, Z)
    units, rows, width = q_buf.shape
    micro = k_win.shape[0]
    per_micro = units // micro
    chunks = rows // CHUNK
    half = chunks // 2
    steps = units * chunks
    slots = Z * CAP * CH
    scale = math.log2(math.e) / math.sqrt(HEAD_WIDTH)

    beside = {"ctx": (1 - x_lo) * Z + z}
    across = {"pipe": 1 - pipe, "ctx": (1 - x_lo) * Z + z}
    right = {"ctx": lax.rem(ctx + 1, ctx_count)}

    def chunk_at(step):
        early = EARLY * half
        later = step - early
        return jnp.where(
            step < early,
            step // half * chunks + lax.rem(step, half),
            jnp.where(
                step < 2 * early,
                later // half * chunks + half + lax.rem(later, half),
                step,
            ),
        )

    def first_row(chunk):
        return pl.multiple_of(lax.rem(chunk + half, chunks) * CHUNK, CHUNK)

    def columns(u):
        return pl.ds(pl.multiple_of(lax.rem(u, per_micro) * width, width), width)

    def q_load(u):
        return pltpu.make_async_copy(
            q_hbm.at[0, u // per_micro, :, columns(u)], q_buf.at[u], q_sem.at[u]
        )

    def starts_load():
        return pltpu.make_async_copy(starts_hbm, starts_ref, small_sem.at[0])

    def owners_load():
        return pltpu.make_async_copy(owners_hbm, owners_ref, small_sem.at[1])

    def kv_load(m, which):
        src, dst = ((k_hbm, k_win), (v_hbm, v_win))[which]
        return pltpu.make_async_copy(
            src.at[0, m],
            dst.at[m, pl.ds(DOCMAX, rows)],
            kv_sem.at[m, which],
        )

    def halo_ends(m, which):
        src, dst = ((k_hbm, k_win), (v_hbm, v_win))[which]
        return (
            src.at[0, m, pl.ds(rows - DOCMAX, DOCMAX)],
            dst.at[m, pl.ds(0, DOCMAX)],
        )

    def halo(m, which):
        src, dst = halo_ends(m, which)
        return pltpu.make_async_remote_copy(
            src_ref=src,
            dst_ref=dst,
            send_sem=halo_send.at[m, which],
            recv_sem=halo_recv.at[m, which],
            device_id=right,
            device_id_type=MESH,
        )

    def relay_z(m, which):
        return (2 * m + which + Z - 1) % Z

    def to_relay(m, which):
        return pltpu.make_async_remote_copy(
            src_ref=halo_ends(m, which)[0],
            dst_ref=relay,
            send_sem=halo_send.at[m, which],
            recv_sem=relay_sem.at[0],
            device_id={"ctx": relay_z(m, which)},
            device_id_type=MESH,
        )

    def from_relay(m, which):
        return pltpu.make_async_remote_copy(
            src_ref=relay,
            dst_ref=halo_ends(m, which)[1],
            send_sem=relay_sem.at[1],
            recv_sem=halo_recv.at[m, which],
            device_id={"ctx": Z},
            device_id_type=MESH,
        )

    def send_halo(m):
        for which in range(2):
            via = relay_z(m, which)
            if via == Z - 1:
                direct = ctx < ctx_count - 1
            else:
                direct = (ctx < ctx_count - 1) & (ctx != Z - 1)

                @pl.when(ctx == Z - 1)
                def _():
                    to_relay(m, which).start()

            @pl.when(direct)
            def _():
                halo(m, which).start()

    def pass_halo(m):
        for which in range(2):
            via = relay_z(m, which)
            if via != Z - 1:

                @pl.when(ctx == via)
                def _():
                    to_relay(m, which).wait_recv()
                    from_relay(m, which).start()

    def dest_copy():
        return pltpu.make_async_remote_copy(
            src_ref=dest.at[0],
            dst_ref=dest.at[1],
            send_sem=dest_sem.at[0],
            recv_sem=dest_sem.at[1],
            device_id=beside,
            device_id_type=MESH,
        )

    def exchange(chunk):
        u, span = chunk // chunks, pl.ds(first_row(chunk), CHUNK)
        return pltpu.make_async_remote_copy(
            src_ref=a_buf.at[u, span],
            dst_ref=b_buf.at[u, span],
            send_sem=all_send.at[0],
            recv_sem=ex_recv.at[chunk],
            device_id=beside,
            device_id_type=MESH,
        )

    def forward(chunk):
        u, span = chunk // chunks, pl.ds(first_row(chunk), CHUNK)
        return pltpu.make_async_remote_copy(
            src_ref=b_buf.at[u, span],
            dst_ref=c_buf.at[u, span],
            send_sem=all_send.at[1],
            recv_sem=fw_recv.at[chunk],
            device_id=across,
            device_id_type=MESH,
        )

    def spread_near(u, z_to, z_from):
        return pltpu.make_async_remote_copy(
            src_ref=s_buf.at[u, :, z_to],
            dst_ref=out_ref.at[u // per_micro, :, z_from, :, :, columns(u)],
            send_sem=all_send.at[2],
            recv_sem=all_recv.at[0],
            device_id={"ctx": x_lo * Z + z_to},
            device_id_type=MESH,
        )

    def keep_near(u):
        return pltpu.make_async_copy(
            s_buf.at[u, :, z],
            out_ref.at[u // per_micro, :, z, :, :, columns(u)],
            all_recv.at[0],
        )

    def spread_far(u, to, source):
        return pltpu.make_async_remote_copy(
            src_ref=s_buf.at[u, to // Z, lax.rem(to, Z)],
            dst_ref=out_ref.at[
                u // per_micro, source // Z, lax.rem(source, Z), :, :, columns(u)
            ],
            send_sem=all_send.at[2],
            recv_sem=all_recv.at[0],
            device_id={"ctx": to},
            device_id_type=MESH,
        )

    def keep_far(u):
        return pltpu.make_async_copy(
            s_buf.at[u, x_lo, z],
            out_ref.at[u // per_micro, x_lo, z, :, :, columns(u)],
            all_recv.at[0],
        )

    barrier = pltpu.get_barrier_semaphore()
    for step in range(1, 2 * Z):
        pl.semaphore_signal(
            barrier,
            inc=1,
            device_id={"ctx": lax.rem(ctx + step, 2 * Z)},
            device_id_type=MESH,
        )
    pl.semaphore_signal(barrier, inc=1, device_id=across, device_id_type=MESH)

    starts_load().start()
    for which in range(2):
        kv_load(0, which).start()
    owners_load().start()

    @pl.loop(0, units)
    def _(u):
        q_load(u).start()

    for which in range(2):
        kv_load(1, which).start()

    def mask_rows(m):
        row_at = lax.broadcasted_iota(jnp.int32, (BLOCK, BLOCK), 0)
        col_at = lax.broadcasted_iota(jnp.int32, (BLOCK, BLOCK), 1)
        for b in range(rows // BLOCK):
            line = starts_ref[pl.ds(m, 1), pl.ds(b * BLOCK, BLOCK)].astype(jnp.float32)
            column = jnp.transpose(jnp.broadcast_to(line, (BLOCK, BLOCK))).astype(jnp.int32)
            first = column - (ctx * rows + b * BLOCK - DOCMAX)
            for part in range(SPAN // BLOCK):
                key_at = col_at + part * BLOCK
                allowed = (key_at >= first) & (key_at <= row_at + DOCMAX)
                bias[m, pl.ds(b * BLOCK, BLOCK), pl.ds(part * BLOCK, BLOCK)] = jnp.where(
                    allowed, 0.0, MASKED
                )

    def find_dest():
        owners_load().wait()
        lane = lax.broadcasted_iota(jnp.int32, (8, rows), 1)
        sub = lax.broadcasted_iota(jnp.int32, (8, rows), 0)
        tract = lax.shift_right_logical(lane, 5)
        slot = jnp.zeros((8, rows), jnp.int32)
        for m in range(micro):
            names = [owners_ref[m, t] for t in range(TRACTS_DEV)]
            for t in range(TRACTS_DEV):
                rank = jnp.int32(0)
                for earlier in range(t):
                    rank = rank + jnp.where(names[earlier] == names[t], 1, 0)
                here = (tract == t) & (sub == m)
                slot = jnp.where(here, names[t] * CAP + rank, slot)
        dest[0] = slot * CH + (lane & (CH - 1))

    def pick_rows(m, whose, at, first, count):
        target = dest[whose, pl.ds(m, 1), :] - first
        wanted = lax.broadcasted_iota(jnp.int32, (count, rows), 0)
        pick[m, pl.ds(at, count), :] = jnp.where(wanted == target, 1.0, 0.0).astype(
            jnp.bfloat16
        )

    def attend(chunk, section):
        u = chunk // chunks
        m = u // per_micro
        base = first_row(chunk)
        spans = [pl.ds(base + b * BLOCK, BLOCK) for b in range(CHUNK // BLOCK)]
        windows = [pl.ds(base + b * BLOCK, SPAN) for b in range(CHUNK // BLOCK)]
        terms = []
        for span, window in zip(spans, windows):
            q = q_buf[u, span, :]
            if section:
                q = (q.astype(jnp.float32) + c_buf[u, span, :].astype(jnp.float32)).astype(
                    jnp.bfloat16
                )
            scores = lax.dot_general(
                q, k_win[m, window, :], (((1,), (1,)), ((), ())), preferred_element_type=jnp.float32
            )
            scores = scores + bias[m, span, :]
            top = jnp.max(scores, axis=1, keepdims=True)
            exps = jnp.exp2((scores - top) * scale)
            terms.append((exps.astype(jnp.bfloat16), jnp.sum(exps, axis=1, keepdims=True)))
        for span, window, (weights, denom) in zip(spans, windows, terms):
            mixed = jnp.dot(weights, v_win[m, window, :], preferred_element_type=jnp.float32)
            a_buf[u, span, :] = (mixed / denom).astype(jnp.bfloat16)

    def await_inputs(chunk):
        u, part = chunk // chunks, lax.rem(chunk, chunks)
        m, g = u // per_micro, lax.rem(u, per_micro)

        @pl.when(part == 0)
        def _():
            q_load(u).wait()

        @pl.when((part == 0) & (g == 0))
        def _():
            for which in range(2):
                kv_load(m, which).wait()

        @pl.when((part == half) & (g == 0) & (ctx > 0))
        def _():
            for which in range(2):
                halo(m, which).wait_recv()

    @pl.when(ctx == 0)
    def _():
        for m in range(micro):
            for window in (k_win, v_win):
                window[m, pl.ds(0, DOCMAX)] = jnp.zeros(
                    (DOCMAX, HEAD_WIDTH), jnp.bfloat16
                )

    starts_load().wait()
    mask_rows(0)

    @pl.when(pipe == 0)
    def _():
        def lead(turn):
            return jnp.minimum(FIRST + turn + jnp.minimum(turn, MORE), steps)

        @pl.loop(0, FIRST)
        def _(step):
            chunk = chunk_at(step)
            await_inputs(chunk)
            attend(chunk, 0)

        pl.semaphore_wait(barrier, 2 * Z)
        send_halo(0)
        for step in range(FIRST):
            exchange(chunk_at(step)).start()

        @pl.loop(0, steps)
        def _(turn):
            @pl.loop(lead(turn), lead(turn + 1))
            def _(step):
                chunk = chunk_at(step)
                await_inputs(chunk)
                attend(chunk, 0)
                exchange(chunk).start()

            chunk = chunk_at(turn)
            u = chunk // chunks
            m = u // per_micro
            exchange(chunk).wait_recv()
            forward(chunk).start()

            @pl.when(lax.rem(chunk, chunks) == chunks - 1)
            def _():
                for place, source, first in ((x_lo, a_buf, 0), (1 - x_lo, b_buf, slots)):
                    picked = jnp.dot(
                        pick[m, pl.ds(first, slots), :],
                        source[u],
                        preferred_element_type=jnp.float32,
                    )
                    s_buf[u, place] = picked.astype(jnp.bfloat16).reshape(Z, CAP, CH, width)
                for to in (2, 1, 3):
                    spread_near(u, lax.rem(z + to, Z), z).start()
                keep_near(u).start()

            @pl.when(turn == half - 1)
            def _():
                pass_halo(0)
                find_dest()
                dest_copy().start()

            @pl.when(turn == 2 * half - 1)
            def _():
                send_halo(1)
                mask_rows(1)

            @pl.when(turn == 4 * half - 1)
            def _():
                pass_halo(1)

            @pl.when(turn == 5 * half)
            def _():
                dest_copy().wait()
                for m in range(micro):
                    for whose in range(2):
                        pick_rows(m, whose, whose * slots, x_lo * slots, slots)

        pltpu.make_async_copy(a_buf, a_buf, all_send.at[0]).wait()
        pltpu.make_async_copy(b_buf, b_buf, all_send.at[1]).wait()
        sent = s_buf.at[pl.ds(0, units - units // Z)]
        pltpu.make_async_copy(sent, sent, all_send.at[2]).wait()

    @pl.when(pipe == 1)
    def _():
        find_dest()
        pl.semaphore_wait(barrier, 2 * Z)
        for m in range(micro):
            send_halo(m)
        for m in range(micro):
            pick_rows(m, 0, 0, 0, 2 * slots)
        mask_rows(1)
        for m in range(micro):
            pass_halo(m)

        @pl.loop(0, steps)
        def _(step):
            chunk = chunk_at(step)
            u = chunk // chunks
            m = u // per_micro
            await_inputs(chunk)
            forward(chunk).wait_recv()
            attend(chunk, 1)

            @pl.when(lax.rem(chunk, chunks) == chunks - 1)
            def _():
                picked = jnp.dot(pick[m], a_buf[u], preferred_element_type=jnp.float32)
                s_buf[u] = picked.astype(jnp.bfloat16).reshape(2, Z, CAP, CH, width)
                for turn in (6, 2, 5, 7, 4, 1, 3):
                    spread_far(u, lax.rem(ctx + turn, 2 * Z), ctx).start()
                keep_far(u).start()

        sent = s_buf.at[pl.ds(0, units - units // (2 * Z))]
        pltpu.make_async_copy(sent, sent, all_send.at[2]).wait()

    pltpu.make_async_copy(out_ref, out_ref, all_recv.at[0]).wait()

    @pl.when(ctx < ctx_count - 1)
    def _():
        for m in range(micro):
            for which in range(2):
                halo(m, which).wait_send()

    for m in range(micro):
        for which in range(2):
            if relay_z(m, which) != Z - 1:

                @pl.when(ctx == relay_z(m, which))
                def _():
                    from_relay(m, which).wait_send()


def local(queries, keys, values, doc_start, owners):
    _, micro, rows, width_q = queries.shape
    unit_width = HEAD_WIDTH
    units = micro * (width_q // unit_width)
    steps = units * (rows // CHUNK)
    bf16, f32, i32 = jnp.bfloat16, jnp.float32, jnp.int32
    dma = pltpu.SemaphoreType.DMA
    in_hbm = pl.BlockSpec(memory_space=pltpu.HBM)
    out = pl.pallas_call(
        kernel,
        out_shape=jax.ShapeDtypeStruct((micro, 2, Z, CAP, CH, width_q), bf16),
        in_specs=[in_hbm] * 5,
        out_specs=pl.BlockSpec(memory_space=pl.ANY),
        scratch_shapes=[
            pltpu.VMEM((units, rows, unit_width), bf16),
            pltpu.VMEM((DOCMAX, HEAD_WIDTH), bf16),
            pltpu.VMEM((units, rows, unit_width), bf16),
            pltpu.VMEM((units, rows, unit_width), bf16),
            pltpu.VMEM((units, rows, unit_width), bf16),
            pltpu.VMEM((units, 2, Z, CAP, CH, unit_width), bf16),
            pltpu.VMEM((micro, DOCMAX + rows, HEAD_WIDTH), bf16),
            pltpu.VMEM((micro, DOCMAX + rows, HEAD_WIDTH), bf16),
            pltpu.VMEM((micro, rows, SPAN), f32),
            pltpu.VMEM((micro, 2 * Z * CAP * CH, rows), bf16),
            pltpu.VMEM((2, 8, rows), i32),
            pltpu.VMEM((micro, rows), i32),
            pltpu.SMEM((micro, TRACTS_DEV), i32),
            dma((2,)),
            dma((units,)),
            dma((micro, 2)),
            dma((micro, 2)),
            dma((micro, 2)),
            dma((2,)),
            dma((2,)),
            dma((steps,)),
            dma((steps,)),
            dma((3,)),
            dma((1,)),
        ],
        compiler_params=pltpu.CompilerParams(
            collective_id=0, has_side_effects=True, vmem_limit_bytes=48 * 1024 * 1024
        ),
    )(*[pltpu.with_memory_space_constraint(a, pltpu.HBM) for a in (queries, keys, values, doc_start, owners)])
    return out.reshape(1, micro, 1, 2 * Z, CAP, CH, width_q)


def solution(mesh):
    return jax.shard_map(
        local,
        mesh=mesh,
        in_specs=(
            P("pipe", None, "ctx", "tp"),
            P("pipe", None, "ctx", "tp"),
            P("pipe", None, "ctx", "tp"),
            P(None, "ctx"),
            P(None, "ctx"),
        ),
        out_specs=P("pipe", None, "ctx", None, None, None, "tp"),
        check_vma=False,
    )
```

```python
import functools
import math

import jax
import jax.numpy as jnp
from jax import lax
from jax.experimental import pallas as pl
from jax.experimental.pallas import tpu as pltpu
from jax.sharding import PartitionSpec as P

HEAD_WIDTH = 128
TRACTS_DEV = 16
CH = 32
CAP = 3
DOCMAX = 256
BLOCK = 128
SPAN = BLOCK + DOCMAX
CHUNK = 256
EARLY = 6
FIRST = 1
MORE = 6
LATE = 4
AHEAD = 2
Z = 4
MESH = pl.DeviceIdType.MESH
MASKED = -1e30


def kernel(
    q_hbm,
    k_hbm,
    v_hbm,
    starts_hbm,
    owners_hbm,
    out_ref,
    q_buf,
    relay,
    c_buf,
    t_buf,
    a_buf,
    b_buf,
    s_buf,
    k_win,
    v_win,
    bias,
    pick,
    dest,
    starts_ref,
    owners_ref,
    small_sem,
    q_sem,
    kv_sem,
    halo_send,
    halo_recv,
    relay_sem,
    dest_sem,
    ex_recv,
    fw_recv,
    cross_recv,
    all_send,
    all_recv,
):
    pipe = lax.axis_index("pipe")
    ctx = lax.axis_index("ctx")
    ctx_count = lax.axis_size("ctx")
    x_lo = ctx // Z
    z = lax.rem(ctx, Z)
    units, rows, width = q_buf.shape
    micro = k_win.shape[0]
    per_micro = units // micro
    chunks = rows // CHUNK
    half = chunks // 2
    steps = units * chunks
    slots = Z * CAP * CH
    scale = math.log2(math.e) / math.sqrt(HEAD_WIDTH)

    beside = {"ctx": (1 - x_lo) * Z + z}
    across = {"pipe": 1 - pipe, "ctx": (1 - x_lo) * Z + z}
    right = {"ctx": lax.rem(ctx + 1, ctx_count)}

    def chunk_at(step, skip):
        early = (EARLY - skip) * half
        later = step - early
        return jnp.where(
            step < early,
            (step // half + skip) * chunks + lax.rem(step, half),
            jnp.where(
                step < 2 * early,
                (later // half + skip) * chunks + half + lax.rem(later, half),
                step + skip * chunks,
            ),
        )

    def first_row(chunk):
        return pl.multiple_of(lax.rem(chunk + half, chunks) * CHUNK, CHUNK)

    def columns(u):
        return pl.ds(pl.multiple_of(lax.rem(u, per_micro) * width, width), width)

    def q_load(u):
        return pltpu.make_async_copy(
            q_hbm.at[0, u // per_micro, :, columns(u)], q_buf.at[u], q_sem.at[u]
        )

    def starts_load():
        return pltpu.make_async_copy(starts_hbm, starts_ref, small_sem.at[0])

    def owners_load():
        return pltpu.make_async_copy(owners_hbm, owners_ref, small_sem.at[1])

    def kv_load(m, which):
        src, dst = ((k_hbm, k_win), (v_hbm, v_win))[which]
        return pltpu.make_async_copy(
            src.at[0, m],
            dst.at[m, pl.ds(DOCMAX, rows)],
            kv_sem.at[m, which],
        )

    def halo_ends(m, which):
        src, dst = ((k_hbm, k_win), (v_hbm, v_win))[which]
        return (
            src.at[0, m, pl.ds(rows - DOCMAX, DOCMAX)],
            dst.at[m, pl.ds(0, DOCMAX)],
        )

    def halo(m, which):
        src, dst = halo_ends(m, which)
        return pltpu.make_async_remote_copy(
            src_ref=src,
            dst_ref=dst,
            send_sem=halo_send.at[m, which],
            recv_sem=halo_recv.at[m, which],
            device_id=right,
            device_id_type=MESH,
        )

    def relay_z(m, which):
        return (2 * m + which + Z - 1) % Z

    def to_relay(m, which):
        return pltpu.make_async_remote_copy(
            src_ref=halo_ends(m, which)[0],
            dst_ref=relay,
            send_sem=halo_send.at[m, which],
            recv_sem=relay_sem.at[0],
            device_id={"ctx": relay_z(m, which)},
            device_id_type=MESH,
        )

    def from_relay(m, which):
        return pltpu.make_async_remote_copy(
            src_ref=relay,
            dst_ref=halo_ends(m, which)[1],
            send_sem=relay_sem.at[1],
            recv_sem=halo_recv.at[m, which],
            device_id={"ctx": Z},
            device_id_type=MESH,
        )

    def send_halo(m):
        for which in range(2):
            via = relay_z(m, which)
            if via == Z - 1:
                direct = ctx < ctx_count - 1
            else:
                direct = (ctx < ctx_count - 1) & (ctx != Z - 1)

                @pl.when(ctx == Z - 1)
                def _():
                    to_relay(m, which).start()

            @pl.when(direct)
            def _():
                halo(m, which).start()

    def pass_halo(m):
        for which in range(2):
            via = relay_z(m, which)
            if via != Z - 1:

                @pl.when(ctx == via)
                def _():
                    to_relay(m, which).wait_recv()
                    from_relay(m, which).start()

    def dest_copy():
        return pltpu.make_async_remote_copy(
            src_ref=dest.at[0],
            dst_ref=dest.at[1],
            send_sem=dest_sem.at[0],
            recv_sem=dest_sem.at[1],
            device_id=beside,
            device_id_type=MESH,
        )

    def exchange(chunk):
        u, span = chunk // chunks, pl.ds(first_row(chunk), CHUNK)
        return pltpu.make_async_remote_copy(
            src_ref=a_buf.at[u, span],
            dst_ref=b_buf.at[u, span],
            send_sem=all_send.at[0],
            recv_sem=ex_recv.at[chunk],
            device_id=beside,
            device_id_type=MESH,
        )

    def forward(chunk):
        u, span = chunk // chunks, pl.ds(first_row(chunk), CHUNK)
        return pltpu.make_async_remote_copy(
            src_ref=b_buf.at[u, span],
            dst_ref=c_buf.at[u, span],
            send_sem=all_send.at[1],
            recv_sem=fw_recv.at[chunk],
            device_id=across,
            device_id_type=MESH,
        )

    def cross(chunk):
        u, span = chunk // chunks, pl.ds(first_row(chunk), CHUNK)
        return pltpu.make_async_remote_copy(
            src_ref=a_buf.at[u, span],
            dst_ref=t_buf.at[u, span],
            send_sem=all_send.at[1],
            recv_sem=cross_recv.at[chunk],
            device_id=across,
            device_id_type=MESH,
        )

    def settle(chunk):
        u, span = chunk // chunks, pl.ds(first_row(chunk), CHUNK)
        return pltpu.make_async_remote_copy(
            src_ref=t_buf.at[u, span],
            dst_ref=c_buf.at[u, span],
            send_sem=all_send.at[0],
            recv_sem=fw_recv.at[chunk],
            device_id=beside,
            device_id_type=MESH,
        )

    def spread_near(u, z_to, z_from):
        return pltpu.make_async_remote_copy(
            src_ref=s_buf.at[u, :, z_to],
            dst_ref=out_ref.at[u // per_micro, :, z_from, :, :, columns(u)],
            send_sem=all_send.at[2],
            recv_sem=all_recv.at[0],
            device_id={"ctx": x_lo * Z + z_to},
            device_id_type=MESH,
        )

    def keep_near(u):
        return pltpu.make_async_copy(
            s_buf.at[u, :, z],
            out_ref.at[u // per_micro, :, z, :, :, columns(u)],
            all_recv.at[0],
        )

    def spread_far(u, to, source):
        return pltpu.make_async_remote_copy(
            src_ref=s_buf.at[u, to // Z, lax.rem(to, Z)],
            dst_ref=out_ref.at[
                u // per_micro, source // Z, lax.rem(source, Z), :, :, columns(u)
            ],
            send_sem=all_send.at[2],
            recv_sem=all_recv.at[0],
            device_id={"ctx": to},
            device_id_type=MESH,
        )

    def keep_far(u):
        return pltpu.make_async_copy(
            s_buf.at[u, x_lo, z],
            out_ref.at[u // per_micro, x_lo, z, :, :, columns(u)],
            all_recv.at[0],
        )

    barrier = pltpu.get_barrier_semaphore()
    for step in range(1, 2 * Z):
        pl.semaphore_signal(
            barrier,
            inc=1,
            device_id={"ctx": lax.rem(ctx + step, 2 * Z)},
            device_id_type=MESH,
        )
    pl.semaphore_signal(barrier, inc=1, device_id=across, device_id_type=MESH)

    starts_load().start()
    for which in range(2):
        kv_load(0, which).start()
    owners_load().start()

    @pl.loop(0, units)
    def _(u):
        q_load(u).start()

    for which in range(2):
        kv_load(1, which).start()

    def mask_rows(m):
        row_at = lax.broadcasted_iota(jnp.int32, (BLOCK, BLOCK), 0)
        col_at = lax.broadcasted_iota(jnp.int32, (BLOCK, BLOCK), 1)
        for b in range(rows // BLOCK):
            line = starts_ref[pl.ds(m, 1), pl.ds(b * BLOCK, BLOCK)].astype(jnp.float32)
            column = jnp.transpose(jnp.broadcast_to(line, (BLOCK, BLOCK))).astype(jnp.int32)
            first = column - (ctx * rows + b * BLOCK - DOCMAX)
            for part in range(SPAN // BLOCK):
                key_at = col_at + part * BLOCK
                allowed = (key_at >= first) & (key_at <= row_at + DOCMAX)
                bias[m, pl.ds(b * BLOCK, BLOCK), pl.ds(part * BLOCK, BLOCK)] = jnp.where(
                    allowed, 0.0, MASKED
                )

    def find_dest():
        owners_load().wait()
        lane = lax.broadcasted_iota(jnp.int32, (8, rows), 1)
        sub = lax.broadcasted_iota(jnp.int32, (8, rows), 0)
        tract = lax.shift_right_logical(lane, 5)
        slot = jnp.zeros((8, rows), jnp.int32)
        for m in range(micro):
            names = [owners_ref[m, t] for t in range(TRACTS_DEV)]
            for t in range(TRACTS_DEV):
                rank = jnp.int32(0)
                for earlier in range(t):
                    rank = rank + jnp.where(names[earlier] == names[t], 1, 0)
                here = (tract == t) & (sub == m)
                slot = jnp.where(here, names[t] * CAP + rank, slot)
        dest[0] = slot * CH + (lane & (CH - 1))

    def pick_rows(m, whose, at, first, count):
        target = dest[whose, pl.ds(m, 1), :] - first
        wanted = lax.broadcasted_iota(jnp.int32, (count, rows), 0)
        pick[m, pl.ds(at, count), :] = jnp.where(wanted == target, 1.0, 0.0).astype(
            jnp.bfloat16
        )

    def attend(chunk, section):
        u = chunk // chunks
        m = u // per_micro
        base = first_row(chunk)
        spans = [pl.ds(base + b * BLOCK, BLOCK) for b in range(CHUNK // BLOCK)]
        windows = [pl.ds(base + b * BLOCK, SPAN) for b in range(CHUNK // BLOCK)]
        terms = []
        for span, window in zip(spans, windows):
            q = q_buf[u, span, :]
            if section:
                q = (q.astype(jnp.float32) + c_buf[u, span, :].astype(jnp.float32)).astype(
                    jnp.bfloat16
                )
            scores = lax.dot_general(
                q, k_win[m, window, :], (((1,), (1,)), ((), ())), preferred_element_type=jnp.float32
            )
            scores = scores + bias[m, span, :]
            top = jnp.max(scores, axis=1, keepdims=True)
            exps = jnp.exp2((scores - top) * scale)
            terms.append((exps.astype(jnp.bfloat16), jnp.sum(exps, axis=1, keepdims=True)))
        for span, window, (weights, denom) in zip(spans, windows, terms):
            mixed = jnp.dot(weights, v_win[m, window, :], preferred_element_type=jnp.float32)
            a_buf[u, span, :] = (mixed / denom).astype(jnp.bfloat16)

    def await_inputs(chunk):
        u, part = chunk // chunks, lax.rem(chunk, chunks)
        m, g = u // per_micro, lax.rem(u, per_micro)

        @pl.when(part == 0)
        def _():
            q_load(u).wait()

        @pl.when((part == 0) & (g == 0))
        def _():
            for which in range(2):
                kv_load(m, which).wait()

        @pl.when((part == half) & (g == 0) & (ctx > 0))
        def _():
            for which in range(2):
                halo(m, which).wait_recv()

    @pl.when(ctx == 0)
    def _():
        for m in range(micro):
            for window in (k_win, v_win):
                window[m, pl.ds(0, DOCMAX)] = jnp.zeros(
                    (DOCMAX, HEAD_WIDTH), jnp.bfloat16
                )

    starts_load().wait()
    mask_rows(0)

    @pl.when(pipe == 0)
    def _():
        turns = steps - AHEAD * chunks

        def lead(turn):
            more = jnp.minimum(jnp.maximum(turn - 1, 0), MORE)
            return jnp.where(
                turn == 0, FIRST, jnp.minimum(FIRST + AHEAD * half + turn + more, steps)
            )

        def launch(chunk):
            @pl.when(chunk < AHEAD * chunks)
            def _():
                cross(chunk).start()

            @pl.when(chunk >= AHEAD * chunks)
            def _():
                exchange(chunk).start()

        def consume(u):
            m = u // per_micro
            for place, source, first in ((x_lo, a_buf, 0), (1 - x_lo, b_buf, slots)):
                picked = jnp.dot(
                    pick[m, pl.ds(first, slots), :],
                    source[u],
                    preferred_element_type=jnp.float32,
                )
                s_buf[u, place] = picked.astype(jnp.bfloat16).reshape(Z, CAP, CH, width)
            for to in (2, 1, 3):
                spread_near(u, lax.rem(z + to, Z), z).start()
            keep_near(u).start()

        @pl.loop(0, FIRST)
        def _(step):
            chunk = chunk_at(step, 0)
            await_inputs(chunk)
            attend(chunk, 0)

        pl.semaphore_wait(barrier, 2 * Z)
        send_halo(0)
        for step in range(FIRST):
            launch(chunk_at(jnp.int32(step), 0))
        find_dest()
        dest_copy().start()

        @pl.loop(0, turns)
        def _(turn):
            @pl.loop(lead(turn), lead(turn + 1))
            def _(step):
                chunk = chunk_at(step, 0)
                await_inputs(chunk)
                attend(chunk, 0)
                launch(chunk)

            chunk = chunk_at(turn, AHEAD)
            exchange(chunk).wait_recv()
            forward(chunk).start()

            @pl.when(lax.rem(chunk, chunks) == chunks - 1)
            def _():
                consume(chunk // chunks)

            @pl.when(turn == 0)
            def _():
                pass_halo(0)

            @pl.when(turn == 1)
            def _():
                send_halo(1)
                dest_copy().wait()
                for m in range(micro):
                    for whose in range(2):
                        pick_rows(m, whose, whose * slots, x_lo * slots, slots)

            @pl.when(turn == 3)
            def _():
                pass_halo(1)
                mask_rows(1)

            @pl.when(turn == turns - LATE)
            def _():
                @pl.loop(0, AHEAD * chunks)
                def _(left):
                    exchange(left).start()

        @pl.loop(0, AHEAD)
        def _(u):
            for part in range(chunks):
                exchange(u * chunks + part).wait_recv()
            consume(u)

        pltpu.make_async_copy(a_buf, a_buf, all_send.at[0]).wait()
        pltpu.make_async_copy(b_buf, b_buf, all_send.at[1]).wait()
        sent = s_buf.at[pl.ds(0, units - units // Z)]
        pltpu.make_async_copy(sent, sent, all_send.at[2]).wait()

    @pl.when(pipe == 1)
    def _():
        find_dest()
        pl.semaphore_wait(barrier, 2 * Z)
        for m in range(micro):
            send_halo(m)
        for m in range(micro):
            pick_rows(m, 0, 0, 0, 2 * slots)
        mask_rows(1)
        for m in range(micro):
            pass_halo(m)

        @pl.loop(0, steps)
        def _(step):
            chunk = chunk_at(step, 0)
            u = chunk // chunks
            m = u // per_micro
            await_inputs(chunk)

            @pl.when(u == 0)
            def _():
                @pl.loop(0, AHEAD)
                def _(other):
                    moved = other * chunks + chunk
                    cross(moved).wait_recv()
                    settle(moved).start()

            forward(chunk).wait_recv()
            attend(chunk, 1)

            @pl.when(lax.rem(chunk, chunks) == chunks - 1)
            def _():
                picked = jnp.dot(pick[m], a_buf[u], preferred_element_type=jnp.float32)
                s_buf[u] = picked.astype(jnp.bfloat16).reshape(2, Z, CAP, CH, width)
                for turn in (6, 2, 5, 7, 4, 1, 3):
                    spread_far(u, lax.rem(ctx + turn, 2 * Z), ctx).start()
                keep_far(u).start()

        pltpu.make_async_copy(t_buf, t_buf, all_send.at[0]).wait()
        sent = s_buf.at[pl.ds(0, units - units // (2 * Z))]
        pltpu.make_async_copy(sent, sent, all_send.at[2]).wait()

    pltpu.make_async_copy(out_ref, out_ref, all_recv.at[0]).wait()

    @pl.when(ctx < ctx_count - 1)
    def _():
        for m in range(micro):
            for which in range(2):
                halo(m, which).wait_send()

    for m in range(micro):
        for which in range(2):
            if relay_z(m, which) != Z - 1:

                @pl.when(ctx == relay_z(m, which))
                def _():
                    from_relay(m, which).wait_send()


def local(queries, keys, values, doc_start, owners):
    _, micro, rows, width_q = queries.shape
    unit_width = HEAD_WIDTH
    units = micro * (width_q // unit_width)
    steps = units * (rows // CHUNK)
    bf16, f32, i32 = jnp.bfloat16, jnp.float32, jnp.int32
    dma = pltpu.SemaphoreType.DMA
    in_hbm = pl.BlockSpec(memory_space=pltpu.HBM)
    out = pl.pallas_call(
        kernel,
        out_shape=jax.ShapeDtypeStruct((micro, 2, Z, CAP, CH, width_q), bf16),
        in_specs=[in_hbm] * 5,
        out_specs=pl.BlockSpec(memory_space=pl.ANY),
        scratch_shapes=[
            pltpu.VMEM((units, rows, unit_width), bf16),
            pltpu.VMEM((DOCMAX, HEAD_WIDTH), bf16),
            pltpu.VMEM((units, rows, unit_width), bf16),
            pltpu.VMEM((AHEAD, rows, unit_width), bf16),
            pltpu.VMEM((units, rows, unit_width), bf16),
            pltpu.VMEM((units, rows, unit_width), bf16),
            pltpu.VMEM((units, 2, Z, CAP, CH, unit_width), bf16),
            pltpu.VMEM((micro, DOCMAX + rows, HEAD_WIDTH), bf16),
            pltpu.VMEM((micro, DOCMAX + rows, HEAD_WIDTH), bf16),
            pltpu.VMEM((micro, rows, SPAN), f32),
            pltpu.VMEM((micro, 2 * Z * CAP * CH, rows), bf16),
            pltpu.VMEM((2, 8, rows), i32),
            pltpu.VMEM((micro, rows), i32),
            pltpu.SMEM((micro, TRACTS_DEV), i32),
            dma((2,)),
            dma((units,)),
            dma((micro, 2)),
            dma((micro, 2)),
            dma((micro, 2)),
            dma((2,)),
            dma((2,)),
            dma((steps,)),
            dma((steps,)),
            dma((AHEAD * (rows // CHUNK),)),
            dma((3,)),
            dma((1,)),
        ],
        compiler_params=pltpu.CompilerParams(
            collective_id=0, has_side_effects=True, vmem_limit_bytes=48 * 1024 * 1024
        ),
    )(*[pltpu.with_memory_space_constraint(a, pltpu.HBM) for a in (queries, keys, values, doc_start, owners)])
    return out.reshape(1, micro, 1, 2 * Z, CAP, CH, width_q)


def solution(mesh):
    return jax.shard_map(
        local,
        mesh=mesh,
        in_specs=(
            P("pipe", None, "ctx", "tp"),
            P("pipe", None, "ctx", "tp"),
            P("pipe", None, "ctx", "tp"),
            P(None, "ctx"),
            P(None, "ctx"),
        ),
        out_specs=P("pipe", None, "ctx", None, None, None, "tp"),
        check_vma=False,
    )
```

```python
import functools
import math

import jax
import jax.numpy as jnp
from jax import lax
from jax.experimental import pallas as pl
from jax.experimental.pallas import tpu as pltpu
from jax.sharding import PartitionSpec as P

HEAD_WIDTH = 128
TRACTS_DEV = 16
CH = 32
CAP = 3
DOCMAX = 256
BLOCK = 128
SPAN = BLOCK + DOCMAX
CHUNK = 256
EARLY = 6
FIRST = 1
MORE = 6
LATE = 4
AHEAD = 2
Z = 4
MESH = pl.DeviceIdType.MESH
MASKED = -1e30


def kernel(
    q_hbm,
    k_hbm,
    v_hbm,
    starts_hbm,
    owners_hbm,
    out_ref,
    q_buf,
    relay,
    c_buf,
    t_buf,
    a_buf,
    b_buf,
    s_buf,
    k_win,
    v_win,
    bias,
    pick,
    dest,
    starts_ref,
    owners_ref,
    small_sem,
    q_sem,
    kv_sem,
    halo_send,
    halo_recv,
    relay_sem,
    dest_sem,
    ex_recv,
    fw_recv,
    cross_recv,
    all_send,
    all_recv,
):
    pipe = lax.axis_index("pipe")
    ctx = lax.axis_index("ctx")
    ctx_count = lax.axis_size("ctx")
    x_lo = ctx // Z
    z = lax.rem(ctx, Z)
    units, rows, width = q_buf.shape
    micro = k_win.shape[0]
    per_micro = units // micro
    chunks = rows // CHUNK
    half = chunks // 2
    steps = units * chunks
    slots = Z * CAP * CH
    scale = math.log2(math.e) / math.sqrt(HEAD_WIDTH)

    beside = {"ctx": (1 - x_lo) * Z + z}
    across = {"pipe": 1 - pipe, "ctx": (1 - x_lo) * Z + z}
    right = {"ctx": lax.rem(ctx + 1, ctx_count)}

    def chunk_at(step, skip):
        early = (EARLY - skip) * half
        later = step - early
        return jnp.where(
            step < early,
            (step // half + skip) * chunks + lax.rem(step, half),
            jnp.where(
                step < 2 * early,
                (later // half + skip) * chunks + half + lax.rem(later, half),
                step + skip * chunks,
            ),
        )

    def first_row(chunk):
        return pl.multiple_of(lax.rem(chunk + half, chunks) * CHUNK, CHUNK)

    def columns(u):
        return pl.ds(pl.multiple_of(lax.rem(u, per_micro) * width, width), width)

    def q_load(u):
        return pltpu.make_async_copy(
            q_hbm.at[0, u // per_micro, :, columns(u)], q_buf.at[u], q_sem.at[u]
        )

    def starts_load():
        return pltpu.make_async_copy(starts_hbm, starts_ref, small_sem.at[0])

    def owners_load():
        return pltpu.make_async_copy(owners_hbm, owners_ref, small_sem.at[1])

    def kv_load(m, which):
        src, dst = ((k_hbm, k_win), (v_hbm, v_win))[which]
        return pltpu.make_async_copy(
            src.at[0, m],
            dst.at[m, pl.ds(DOCMAX, rows)],
            kv_sem.at[m, which],
        )

    def halo_ends(m, which):
        src, dst = ((k_hbm, k_win), (v_hbm, v_win))[which]
        return (
            src.at[0, m, pl.ds(rows - DOCMAX, DOCMAX)],
            dst.at[m, pl.ds(0, DOCMAX)],
        )

    def halo(m, which):
        src, dst = halo_ends(m, which)
        return pltpu.make_async_remote_copy(
            src_ref=src,
            dst_ref=dst,
            send_sem=halo_send.at[m, which],
            recv_sem=halo_recv.at[m, which],
            device_id=right,
            device_id_type=MESH,
        )

    def relay_z(m, which):
        return (2 * m + which + Z - 1) % Z

    def to_relay(m, which):
        return pltpu.make_async_remote_copy(
            src_ref=halo_ends(m, which)[0],
            dst_ref=relay,
            send_sem=halo_send.at[m, which],
            recv_sem=relay_sem.at[0],
            device_id={"ctx": relay_z(m, which)},
            device_id_type=MESH,
        )

    def from_relay(m, which):
        return pltpu.make_async_remote_copy(
            src_ref=relay,
            dst_ref=halo_ends(m, which)[1],
            send_sem=relay_sem.at[1],
            recv_sem=halo_recv.at[m, which],
            device_id={"ctx": Z},
            device_id_type=MESH,
        )

    def send_halo(m):
        for which in range(2):
            via = relay_z(m, which)
            if via == Z - 1:
                direct = ctx < ctx_count - 1
            else:
                direct = (ctx < ctx_count - 1) & (ctx != Z - 1)

                @pl.when(ctx == Z - 1)
                def _():
                    to_relay(m, which).start()

            @pl.when(direct)
            def _():
                halo(m, which).start()

    def pass_halo(m):
        for which in range(2):
            via = relay_z(m, which)
            if via != Z - 1:

                @pl.when(ctx == via)
                def _():
                    to_relay(m, which).wait_recv()
                    from_relay(m, which).start()

    def dest_copy():
        return pltpu.make_async_remote_copy(
            src_ref=dest.at[0],
            dst_ref=dest.at[1],
            send_sem=dest_sem.at[0],
            recv_sem=dest_sem.at[1],
            device_id=beside,
            device_id_type=MESH,
        )

    def exchange(chunk):
        u, span = chunk // chunks, pl.ds(first_row(chunk), CHUNK)
        return pltpu.make_async_remote_copy(
            src_ref=a_buf.at[u, span],
            dst_ref=b_buf.at[u, span],
            send_sem=all_send.at[0],
            recv_sem=ex_recv.at[chunk],
            device_id=beside,
            device_id_type=MESH,
        )

    def forward(chunk):
        u, span = chunk // chunks, pl.ds(first_row(chunk), CHUNK)
        return pltpu.make_async_remote_copy(
            src_ref=b_buf.at[u, span],
            dst_ref=c_buf.at[u, span],
            send_sem=all_send.at[1],
            recv_sem=fw_recv.at[chunk],
            device_id=across,
            device_id_type=MESH,
        )

    def cross(chunk):
        u, span = chunk // chunks, pl.ds(first_row(chunk), CHUNK)
        return pltpu.make_async_remote_copy(
            src_ref=a_buf.at[u, span],
            dst_ref=t_buf.at[u, span],
            send_sem=all_send.at[1],
            recv_sem=cross_recv.at[chunk],
            device_id=across,
            device_id_type=MESH,
        )

    def settle(chunk):
        u, span = chunk // chunks, pl.ds(first_row(chunk), CHUNK)
        return pltpu.make_async_remote_copy(
            src_ref=t_buf.at[u, span],
            dst_ref=c_buf.at[u, span],
            send_sem=all_send.at[0],
            recv_sem=fw_recv.at[chunk],
            device_id=beside,
            device_id_type=MESH,
        )

    def spread_near(u, z_to, z_from):
        return pltpu.make_async_remote_copy(
            src_ref=s_buf.at[u, :, z_to],
            dst_ref=out_ref.at[u // per_micro, :, z_from, :, :, columns(u)],
            send_sem=all_send.at[2],
            recv_sem=all_recv.at[0],
            device_id={"ctx": x_lo * Z + z_to},
            device_id_type=MESH,
        )

    def keep_near(u):
        return pltpu.make_async_copy(
            s_buf.at[u, :, z],
            out_ref.at[u // per_micro, :, z, :, :, columns(u)],
            all_recv.at[0],
        )

    def spread_far(u, to, source):
        return pltpu.make_async_remote_copy(
            src_ref=s_buf.at[u, to // Z, lax.rem(to, Z)],
            dst_ref=out_ref.at[
                u // per_micro, source // Z, lax.rem(source, Z), :, :, columns(u)
            ],
            send_sem=all_send.at[2],
            recv_sem=all_recv.at[0],
            device_id={"ctx": to},
            device_id_type=MESH,
        )

    def keep_far(u):
        return pltpu.make_async_copy(
            s_buf.at[u, x_lo, z],
            out_ref.at[u // per_micro, x_lo, z, :, :, columns(u)],
            all_recv.at[0],
        )

    barrier = pltpu.get_barrier_semaphore()
    for step in range(1, 2 * Z):
        pl.semaphore_signal(
            barrier,
            inc=1,
            device_id={"ctx": lax.rem(ctx + step, 2 * Z)},
            device_id_type=MESH,
        )
    pl.semaphore_signal(barrier, inc=1, device_id=across, device_id_type=MESH)

    starts_load().start()
    for which in range(2):
        kv_load(0, which).start()
    owners_load().start()

    @pl.loop(0, units)
    def _(u):
        q_load(u).start()

    for which in range(2):
        kv_load(1, which).start()

    def mask_rows(m):
        row_at = lax.broadcasted_iota(jnp.int32, (BLOCK, BLOCK), 0)
        col_at = lax.broadcasted_iota(jnp.int32, (BLOCK, BLOCK), 1)
        for b in range(rows // BLOCK):
            line = starts_ref[pl.ds(m, 1), pl.ds(b * BLOCK, BLOCK)].astype(jnp.float32)
            column = jnp.transpose(jnp.broadcast_to(line, (BLOCK, BLOCK))).astype(jnp.int32)
            first = column - (ctx * rows + b * BLOCK - DOCMAX)
            for part in range(SPAN // BLOCK):
                key_at = col_at + part * BLOCK
                allowed = (key_at >= first) & (key_at <= row_at + DOCMAX)
                bias[m, pl.ds(b * BLOCK, BLOCK), pl.ds(part * BLOCK, BLOCK)] = jnp.where(
                    allowed, 0.0, MASKED
                )

    def find_dest():
        owners_load().wait()
        lane = lax.broadcasted_iota(jnp.int32, (8, rows), 1)
        sub = lax.broadcasted_iota(jnp.int32, (8, rows), 0)
        tract = lax.shift_right_logical(lane, 5)
        slot = jnp.zeros((8, rows), jnp.int32)
        for m in range(micro):
            names = [owners_ref[m, t] for t in range(TRACTS_DEV)]
            for t in range(TRACTS_DEV):
                rank = jnp.int32(0)
                for earlier in range(t):
                    rank = rank + jnp.where(names[earlier] == names[t], 1, 0)
                here = (tract == t) & (sub == m)
                slot = jnp.where(here, names[t] * CAP + rank, slot)
        dest[0] = slot * CH + (lane & (CH - 1))

    def pick_rows(m, whose, at, first, count):
        target = dest[whose, pl.ds(m, 1), :] - first
        wanted = lax.broadcasted_iota(jnp.int32, (count, rows), 0)
        pick[m, pl.ds(at, count), :] = jnp.where(wanted == target, 1.0, 0.0).astype(
            jnp.bfloat16
        )

    def attend(chunk, section):
        u = chunk // chunks
        m = u // per_micro
        base = first_row(chunk)
        spans = [pl.ds(base + b * BLOCK, BLOCK) for b in range(CHUNK // BLOCK)]
        windows = [pl.ds(base + b * BLOCK, SPAN) for b in range(CHUNK // BLOCK)]
        terms = []
        for span, window in zip(spans, windows):
            q = q_buf[u, span, :]
            if section:
                q = (q.astype(jnp.float32) + c_buf[u, span, :].astype(jnp.float32)).astype(
                    jnp.bfloat16
                )
            scores = lax.dot_general(
                q, k_win[m, window, :], (((1,), (1,)), ((), ())), preferred_element_type=jnp.float32
            )
            scores = scores + bias[m, span, :]
            top = jnp.max(scores, axis=1, keepdims=True)
            exps = jnp.exp2((scores - top) * scale)
            terms.append((exps.astype(jnp.bfloat16), jnp.sum(exps, axis=1, keepdims=True)))
        for span, window, (weights, denom) in zip(spans, windows, terms):
            mixed = jnp.dot(weights, v_win[m, window, :], preferred_element_type=jnp.float32)
            a_buf[u, span, :] = (mixed / denom).astype(jnp.bfloat16)

    def await_inputs(chunk):
        u, part = chunk // chunks, lax.rem(chunk, chunks)
        m, g = u // per_micro, lax.rem(u, per_micro)

        @pl.when(part == 0)
        def _():
            q_load(u).wait()

        @pl.when((part == 0) & (g == 0))
        def _():
            for which in range(2):
                kv_load(m, which).wait()

        @pl.when((part == half) & (g == 0) & (ctx > 0))
        def _():
            for which in range(2):
                halo(m, which).wait_recv()

    @pl.when(ctx == 0)
    def _():
        for m in range(micro):
            for window in (k_win, v_win):
                window[m, pl.ds(0, DOCMAX)] = jnp.zeros(
                    (DOCMAX, HEAD_WIDTH), jnp.bfloat16
                )

    starts_load().wait()
    mask_rows(0)

    @pl.when(pipe == 0)
    def _():
        turns = steps - AHEAD * chunks

        def lead(turn):
            more = jnp.minimum(jnp.maximum(turn - 1, 0), MORE)
            return jnp.where(
                turn == 0, FIRST, jnp.minimum(FIRST + AHEAD * half + turn + more, steps)
            )

        def launch(chunk):
            @pl.when(chunk < AHEAD * chunks)
            def _():
                cross(chunk).start()

            @pl.when(chunk >= AHEAD * chunks)
            def _():
                exchange(chunk).start()

        def consume(u):
            m = u // per_micro
            for place, source, first in ((x_lo, a_buf, 0), (1 - x_lo, b_buf, slots)):
                picked = jnp.dot(
                    pick[m, pl.ds(first, slots), :],
                    source[u],
                    preferred_element_type=jnp.float32,
                )
                s_buf[u, place] = picked.astype(jnp.bfloat16).reshape(Z, CAP, CH, width)
            for to in (2, 1, 3):
                spread_near(u, lax.rem(z + to, Z), z).start()
            keep_near(u).start()

        @pl.loop(0, FIRST)
        def _(step):
            chunk = chunk_at(step, 0)
            await_inputs(chunk)
            attend(chunk, 0)

        pl.semaphore_wait(barrier, 2 * Z)
        send_halo(0)
        send_halo(1)
        for step in range(FIRST):
            launch(chunk_at(jnp.int32(step), 0))
        find_dest()
        dest_copy().start()

        @pl.loop(0, turns)
        def _(turn):
            @pl.loop(lead(turn), lead(turn + 1))
            def _(step):
                chunk = chunk_at(step, 0)
                await_inputs(chunk)
                attend(chunk, 0)
                launch(chunk)

            chunk = chunk_at(turn, AHEAD)
            exchange(chunk).wait_recv()
            forward(chunk).start()

            @pl.when(lax.rem(chunk, chunks) == chunks - 1)
            def _():
                consume(chunk // chunks)

            @pl.when(turn == 0)
            def _():
                pass_halo(0)

            @pl.when(turn == 1)
            def _():
                dest_copy().wait()
                for m in range(micro):
                    for whose in range(2):
                        pick_rows(m, whose, whose * slots, x_lo * slots, slots)

            @pl.when(turn == 2)
            def _():
                pass_halo(1)
                mask_rows(1)

            @pl.when(turn == turns - LATE)
            def _():
                @pl.loop(0, AHEAD * chunks)
                def _(left):
                    exchange(left).start()

        @pl.loop(0, AHEAD)
        def _(u):
            for part in range(chunks):
                exchange(u * chunks + part).wait_recv()
            consume(u)

        pltpu.make_async_copy(a_buf, a_buf, all_send.at[0]).wait()
        pltpu.make_async_copy(b_buf, b_buf, all_send.at[1]).wait()
        sent = s_buf.at[pl.ds(0, units - units // Z)]
        pltpu.make_async_copy(sent, sent, all_send.at[2]).wait()

    @pl.when(pipe == 1)
    def _():
        find_dest()
        pl.semaphore_wait(barrier, 2 * Z)
        for m in range(micro):
            send_halo(m)
        for m in range(micro):
            pick_rows(m, 0, 0, 0, 2 * slots)
        mask_rows(1)
        for m in range(micro):
            pass_halo(m)

        @pl.loop(0, steps)
        def _(step):
            chunk = chunk_at(step, 0)
            u = chunk // chunks
            m = u // per_micro
            await_inputs(chunk)

            @pl.when(u == 0)
            def _():
                @pl.loop(0, AHEAD)
                def _(other):
                    moved = other * chunks + chunk
                    cross(moved).wait_recv()
                    settle(moved).start()

            forward(chunk).wait_recv()
            attend(chunk, 1)

            @pl.when(lax.rem(chunk, chunks) == chunks - 1)
            def _():
                picked = jnp.dot(pick[m], a_buf[u], preferred_element_type=jnp.float32)
                s_buf[u] = picked.astype(jnp.bfloat16).reshape(2, Z, CAP, CH, width)
                for other_x, turn in ((1, 2), (1, 1), (1, 3), (1, 0), (0, 2), (0, 1), (0, 3)):
                    place = x_lo if other_x == 0 else 1 - x_lo
                    spread_far(u, place * Z + lax.rem(z + turn, Z), ctx).start()
                keep_far(u).start()

        pltpu.make_async_copy(t_buf, t_buf, all_send.at[0]).wait()
        sent = s_buf.at[pl.ds(0, units - units // (2 * Z))]
        pltpu.make_async_copy(sent, sent, all_send.at[2]).wait()

    pltpu.make_async_copy(out_ref, out_ref, all_recv.at[0]).wait()

    @pl.when(ctx < ctx_count - 1)
    def _():
        for m in range(micro):
            for which in range(2):
                halo(m, which).wait_send()

    for m in range(micro):
        for which in range(2):
            if relay_z(m, which) != Z - 1:

                @pl.when(ctx == relay_z(m, which))
                def _():
                    from_relay(m, which).wait_send()


def local(queries, keys, values, doc_start, owners):
    _, micro, rows, width_q = queries.shape
    unit_width = HEAD_WIDTH
    units = micro * (width_q // unit_width)
    steps = units * (rows // CHUNK)
    bf16, f32, i32 = jnp.bfloat16, jnp.float32, jnp.int32
    dma = pltpu.SemaphoreType.DMA
    in_hbm = pl.BlockSpec(memory_space=pltpu.HBM)
    out = pl.pallas_call(
        kernel,
        out_shape=jax.ShapeDtypeStruct((micro, 2, Z, CAP, CH, width_q), bf16),
        in_specs=[in_hbm] * 5,
        out_specs=pl.BlockSpec(memory_space=pl.ANY),
        scratch_shapes=[
            pltpu.VMEM((units, rows, unit_width), bf16),
            pltpu.VMEM((DOCMAX, HEAD_WIDTH), bf16),
            pltpu.VMEM((units, rows, unit_width), bf16),
            pltpu.VMEM((AHEAD, rows, unit_width), bf16),
            pltpu.VMEM((units, rows, unit_width), bf16),
            pltpu.VMEM((units, rows, unit_width), bf16),
            pltpu.VMEM((units, 2, Z, CAP, CH, unit_width), bf16),
            pltpu.VMEM((micro, DOCMAX + rows, HEAD_WIDTH), bf16),
            pltpu.VMEM((micro, DOCMAX + rows, HEAD_WIDTH), bf16),
            pltpu.VMEM((micro, rows, SPAN), f32),
            pltpu.VMEM((micro, 2 * Z * CAP * CH, rows), bf16),
            pltpu.VMEM((2, 8, rows), i32),
            pltpu.VMEM((micro, rows), i32),
            pltpu.SMEM((micro, TRACTS_DEV), i32),
            dma((2,)),
            dma((units,)),
            dma((micro, 2)),
            dma((micro, 2)),
            dma((micro, 2)),
            dma((2,)),
            dma((2,)),
            dma((steps,)),
            dma((steps,)),
            dma((AHEAD * (rows // CHUNK),)),
            dma((3,)),
            dma((1,)),
        ],
        compiler_params=pltpu.CompilerParams(
            collective_id=0, has_side_effects=True, vmem_limit_bytes=48 * 1024 * 1024
        ),
    )(*[pltpu.with_memory_space_constraint(a, pltpu.HBM) for a in (queries, keys, values, doc_start, owners)])
    return out.reshape(1, micro, 1, 2 * Z, CAP, CH, width_q)


def solution(mesh):
    return jax.shard_map(
        local,
        mesh=mesh,
        in_specs=(
            P("pipe", None, "ctx", "tp"),
            P("pipe", None, "ctx", "tp"),
            P("pipe", None, "ctx", "tp"),
            P(None, "ctx"),
            P(None, "ctx"),
        ),
        out_specs=P("pipe", None, "ctx", None, None, None, "tp"),
        check_vma=False,
    )
```

```python
import functools
import math

import jax
import jax.numpy as jnp
from jax import lax
from jax.experimental import pallas as pl
from jax.experimental.pallas import tpu as pltpu
from jax.sharding import PartitionSpec as P

HEAD_WIDTH = 128
TRACTS_DEV = 16
CH = 32
CAP = 3
DOCMAX = 256
BLOCK = 128
SPAN = BLOCK + DOCMAX
CHUNK = 256
EARLY = 6
FIRST = 1
MORE = 6
LATE = 4
AHEAD = 2
Z = 4
MESH = pl.DeviceIdType.MESH
MASKED = -1e30


def kernel(
    q_hbm,
    k_hbm,
    v_hbm,
    starts_hbm,
    owners_hbm,
    out_ref,
    q_buf,
    relay,
    c_buf,
    t_buf,
    a_buf,
    b_buf,
    s_buf,
    k_win,
    v_win,
    bias,
    pick,
    dest,
    starts_ref,
    owners_ref,
    small_sem,
    q_sem,
    kv_sem,
    halo_send,
    halo_recv,
    relay_sem,
    dest_sem,
    ex_recv,
    fw_recv,
    cross_recv,
    all_send,
    all_recv,
):
    pipe = lax.axis_index("pipe")
    ctx = lax.axis_index("ctx")
    ctx_count = lax.axis_size("ctx")
    x_lo = ctx // Z
    z = lax.rem(ctx, Z)
    units, rows, width = q_buf.shape
    micro = k_win.shape[0]
    per_micro = units // micro
    chunks = rows // CHUNK
    half = chunks // 2
    steps = units * chunks
    slots = Z * CAP * CH
    scale = math.log2(math.e) / math.sqrt(HEAD_WIDTH)

    beside = {"ctx": (1 - x_lo) * Z + z}
    across = {"pipe": 1 - pipe, "ctx": (1 - x_lo) * Z + z}
    right = {"ctx": lax.rem(ctx + 1, ctx_count)}

    def chunk_at(step, skip):
        early = (EARLY - skip) * half
        later = step - early
        return jnp.where(
            step < early,
            (step // half + skip) * chunks + lax.rem(step, half),
            jnp.where(
                step < 2 * early,
                (later // half + skip) * chunks + half + lax.rem(later, half),
                step + skip * chunks,
            ),
        )

    def first_row(chunk):
        return pl.multiple_of(lax.rem(chunk + half, chunks) * CHUNK, CHUNK)

    def columns(u):
        return pl.ds(pl.multiple_of(lax.rem(u, per_micro) * width, width), width)

    def q_load(u):
        return pltpu.make_async_copy(
            q_hbm.at[0, u // per_micro, :, columns(u)], q_buf.at[u], q_sem.at[u]
        )

    def starts_load():
        return pltpu.make_async_copy(starts_hbm, starts_ref, small_sem.at[0])

    def owners_load():
        return pltpu.make_async_copy(owners_hbm, owners_ref, small_sem.at[1])

    def kv_load(m, which):
        src, dst = ((k_hbm, k_win), (v_hbm, v_win))[which]
        return pltpu.make_async_copy(
            src.at[0, m],
            dst.at[m, pl.ds(DOCMAX, rows)],
            kv_sem.at[m, which],
        )

    def halo_ends(m, which):
        src, dst = ((k_hbm, k_win), (v_hbm, v_win))[which]
        return (
            src.at[0, m, pl.ds(rows - DOCMAX, DOCMAX)],
            dst.at[m, pl.ds(0, DOCMAX)],
        )

    def halo(m, which):
        src, dst = halo_ends(m, which)
        return pltpu.make_async_remote_copy(
            src_ref=src,
            dst_ref=dst,
            send_sem=halo_send.at[m, which],
            recv_sem=halo_recv.at[m, which],
            device_id=right,
            device_id_type=MESH,
        )

    def relay_z(m, which):
        return (2 * m + which + Z - 1) % Z

    def to_relay(m, which):
        return pltpu.make_async_remote_copy(
            src_ref=halo_ends(m, which)[0],
            dst_ref=relay,
            send_sem=halo_send.at[m, which],
            recv_sem=relay_sem.at[0],
            device_id={"ctx": relay_z(m, which)},
            device_id_type=MESH,
        )

    def from_relay(m, which):
        return pltpu.make_async_remote_copy(
            src_ref=relay,
            dst_ref=halo_ends(m, which)[1],
            send_sem=relay_sem.at[1],
            recv_sem=halo_recv.at[m, which],
            device_id={"ctx": Z},
            device_id_type=MESH,
        )

    def send_halo(m):
        for which in range(2):
            via = relay_z(m, which)
            if via == Z - 1:
                direct = ctx < ctx_count - 1
            else:
                direct = (ctx < ctx_count - 1) & (ctx != Z - 1)

                @pl.when(ctx == Z - 1)
                def _():
                    to_relay(m, which).start()

            @pl.when(direct)
            def _():
                halo(m, which).start()

    def pass_halo(m):
        for which in range(2):
            via = relay_z(m, which)
            if via != Z - 1:

                @pl.when(ctx == via)
                def _():
                    to_relay(m, which).wait_recv()
                    from_relay(m, which).start()

    def dest_copy():
        return pltpu.make_async_remote_copy(
            src_ref=dest.at[0],
            dst_ref=dest.at[1],
            send_sem=dest_sem.at[0],
            recv_sem=dest_sem.at[1],
            device_id=beside,
            device_id_type=MESH,
        )

    def exchange(chunk):
        u, span = chunk // chunks, pl.ds(first_row(chunk), CHUNK)
        return pltpu.make_async_remote_copy(
            src_ref=a_buf.at[u, span],
            dst_ref=b_buf.at[u, span],
            send_sem=all_send.at[0],
            recv_sem=ex_recv.at[chunk],
            device_id=beside,
            device_id_type=MESH,
        )

    def forward(chunk):
        u, span = chunk // chunks, pl.ds(first_row(chunk), CHUNK)
        return pltpu.make_async_remote_copy(
            src_ref=b_buf.at[u, span],
            dst_ref=c_buf.at[u, span],
            send_sem=all_send.at[1],
            recv_sem=fw_recv.at[chunk],
            device_id=across,
            device_id_type=MESH,
        )

    def cross(chunk):
        u, span = chunk // chunks, pl.ds(first_row(chunk), CHUNK)
        return pltpu.make_async_remote_copy(
            src_ref=a_buf.at[u, span],
            dst_ref=t_buf.at[u, span],
            send_sem=all_send.at[1],
            recv_sem=cross_recv.at[chunk],
            device_id=across,
            device_id_type=MESH,
        )

    def settle(chunk):
        u, span = chunk // chunks, pl.ds(first_row(chunk), CHUNK)
        return pltpu.make_async_remote_copy(
            src_ref=t_buf.at[u, span],
            dst_ref=c_buf.at[u, span],
            send_sem=all_send.at[0],
            recv_sem=fw_recv.at[chunk],
            device_id=beside,
            device_id_type=MESH,
        )

    def spread_near(u, z_to, z_from):
        return pltpu.make_async_remote_copy(
            src_ref=s_buf.at[u, :, z_to],
            dst_ref=out_ref.at[u // per_micro, :, z_from, :, :, columns(u)],
            send_sem=all_send.at[2],
            recv_sem=all_recv.at[0],
            device_id={"ctx": x_lo * Z + z_to},
            device_id_type=MESH,
        )

    def keep_near(u):
        return pltpu.make_async_copy(
            s_buf.at[u, :, z],
            out_ref.at[u // per_micro, :, z, :, :, columns(u)],
            all_recv.at[0],
        )

    def spread_far(u, to, source):
        return pltpu.make_async_remote_copy(
            src_ref=s_buf.at[u, to // Z, lax.rem(to, Z)],
            dst_ref=out_ref.at[
                u // per_micro, source // Z, lax.rem(source, Z), :, :, columns(u)
            ],
            send_sem=all_send.at[2],
            recv_sem=all_recv.at[0],
            device_id={"ctx": to},
            device_id_type=MESH,
        )

    def keep_far(u):
        return pltpu.make_async_copy(
            s_buf.at[u, x_lo, z],
            out_ref.at[u // per_micro, x_lo, z, :, :, columns(u)],
            all_recv.at[0],
        )

    barrier = pltpu.get_barrier_semaphore()
    for step in range(1, 2 * Z):
        pl.semaphore_signal(
            barrier,
            inc=1,
            device_id={"ctx": lax.rem(ctx + step, 2 * Z)},
            device_id_type=MESH,
        )
    pl.semaphore_signal(barrier, inc=1, device_id=across, device_id_type=MESH)

    starts_load().start()
    for which in range(2):
        kv_load(0, which).start()
    owners_load().start()

    @pl.loop(0, units)
    def _(u):
        q_load(u).start()

    for which in range(2):
        kv_load(1, which).start()

    def mask_rows(m):
        row_at = lax.broadcasted_iota(jnp.int32, (BLOCK, BLOCK), 0)
        col_at = lax.broadcasted_iota(jnp.int32, (BLOCK, BLOCK), 1)
        for b in range(rows // BLOCK):
            line = starts_ref[pl.ds(m, 1), pl.ds(b * BLOCK, BLOCK)].astype(jnp.float32)
            column = jnp.transpose(jnp.broadcast_to(line, (BLOCK, BLOCK))).astype(jnp.int32)
            first = column - (ctx * rows + b * BLOCK - DOCMAX)
            for part in range(SPAN // BLOCK):
                key_at = col_at + part * BLOCK
                allowed = (key_at >= first) & (key_at <= row_at + DOCMAX)
                bias[m, pl.ds(b * BLOCK, BLOCK), pl.ds(part * BLOCK, BLOCK)] = jnp.where(
                    allowed, 0.0, MASKED
                )

    def find_dest():
        owners_load().wait()
        lane = lax.broadcasted_iota(jnp.int32, (8, rows), 1)
        sub = lax.broadcasted_iota(jnp.int32, (8, rows), 0)
        tract = lax.shift_right_logical(lane, 5)
        slot = jnp.zeros((8, rows), jnp.int32)
        for m in range(micro):
            names = [owners_ref[m, t] for t in range(TRACTS_DEV)]
            for t in range(TRACTS_DEV):
                rank = jnp.int32(0)
                for earlier in range(t):
                    rank = rank + jnp.where(names[earlier] == names[t], 1, 0)
                here = (tract == t) & (sub == m)
                slot = jnp.where(here, names[t] * CAP + rank, slot)
        dest[0] = slot * CH + (lane & (CH - 1))

    def pick_rows(m, whose, at, first, count):
        target = dest[whose, pl.ds(m, 1), :] - first
        wanted = lax.broadcasted_iota(jnp.int32, (count, rows), 0)
        pick[m, pl.ds(at, count), :] = jnp.where(wanted == target, 1.0, 0.0).astype(
            jnp.bfloat16
        )

    def attend(chunk, section):
        u = chunk // chunks
        m = u // per_micro
        base = first_row(chunk)
        spans = [pl.ds(base + b * BLOCK, BLOCK) for b in range(CHUNK // BLOCK)]
        windows = [pl.ds(base + b * BLOCK, SPAN) for b in range(CHUNK // BLOCK)]
        terms = []
        for span, window in zip(spans, windows):
            q = q_buf[u, span, :]
            if section:
                q = (q.astype(jnp.float32) + c_buf[u, span, :].astype(jnp.float32)).astype(
                    jnp.bfloat16
                )
            scores = lax.dot_general(
                q, k_win[m, window, :], (((1,), (1,)), ((), ())), preferred_element_type=jnp.float32
            )
            scores = scores + bias[m, span, :]
            top = jnp.max(scores, axis=1, keepdims=True)
            exps = jnp.exp2((scores - top) * scale)
            terms.append((exps.astype(jnp.bfloat16), jnp.sum(exps, axis=1, keepdims=True)))
        for span, window, (weights, denom) in zip(spans, windows, terms):
            mixed = jnp.dot(weights, v_win[m, window, :], preferred_element_type=jnp.float32)
            a_buf[u, span, :] = (mixed / denom).astype(jnp.bfloat16)

    def await_inputs(chunk):
        u, part = chunk // chunks, lax.rem(chunk, chunks)
        m, g = u // per_micro, lax.rem(u, per_micro)

        @pl.when(part == 0)
        def _():
            q_load(u).wait()

        @pl.when((part == 0) & (g == 0))
        def _():
            for which in range(2):
                kv_load(m, which).wait()

        @pl.when((part == half) & (g == 0) & (ctx > 0))
        def _():
            for which in range(2):
                halo(m, which).wait_recv()

    @pl.when(ctx == 0)
    def _():
        for m in range(micro):
            for window in (k_win, v_win):
                window[m, pl.ds(0, DOCMAX)] = jnp.zeros(
                    (DOCMAX, HEAD_WIDTH), jnp.bfloat16
                )

    starts_load().wait()
    mask_rows(0)

    @pl.when(pipe == 0)
    def _():
        turns = steps - AHEAD * chunks

        def lead(turn):
            more = jnp.minimum(jnp.maximum(turn - 1, 0), MORE)
            return jnp.where(
                turn == 0, FIRST, jnp.minimum(FIRST + AHEAD * half + turn + more, steps)
            )

        def launch(chunk):
            @pl.when(chunk < AHEAD * chunks)
            def _():
                cross(chunk).start()

            @pl.when(chunk >= AHEAD * chunks)
            def _():
                exchange(chunk).start()

        def consume(u):
            m = u // per_micro
            for place, source, first in ((x_lo, a_buf, 0), (1 - x_lo, b_buf, slots)):
                picked = jnp.dot(
                    pick[m, pl.ds(first, slots), :],
                    source[u],
                    preferred_element_type=jnp.float32,
                )
                s_buf[u, place] = picked.astype(jnp.bfloat16).reshape(Z, CAP, CH, width)
            for to in (2, 1, 3):
                spread_near(u, lax.rem(z + to, Z), z).start()
            keep_near(u).start()

        @pl.loop(0, FIRST)
        def _(step):
            chunk = chunk_at(step, 0)
            await_inputs(chunk)
            attend(chunk, 0)

        pl.semaphore_wait(barrier, 2 * Z)
        send_halo(0)
        send_halo(1)
        for step in range(FIRST):
            launch(chunk_at(jnp.int32(step), 0))
        find_dest()
        dest_copy().start()

        @pl.loop(0, turns)
        def _(turn):
            @pl.loop(lead(turn), lead(turn + 1))
            def _(step):
                chunk = chunk_at(step, 0)
                await_inputs(chunk)
                attend(chunk, 0)
                launch(chunk)

            chunk = chunk_at(turn, AHEAD)
            exchange(chunk).wait_recv()
            forward(chunk).start()

            @pl.when(lax.rem(chunk, chunks) == chunks - 1)
            def _():
                consume(chunk // chunks)

            @pl.when(turn == 0)
            def _():
                pass_halo(0)

            @pl.when(turn == 1)
            def _():
                dest_copy().wait()
                for m in range(micro):
                    for whose in range(2):
                        pick_rows(m, whose, whose * slots, x_lo * slots, slots)

            @pl.when(turn == 2)
            def _():
                pass_halo(1)
                mask_rows(1)

            @pl.when(turn == turns - LATE)
            def _():
                @pl.loop(0, AHEAD * chunks)
                def _(left):
                    exchange(left).start()

        @pl.loop(0, AHEAD)
        def _(u):
            for part in range(chunks):
                exchange(u * chunks + part).wait_recv()
            consume(u)

        pltpu.make_async_copy(a_buf, a_buf, all_send.at[0]).wait()
        pltpu.make_async_copy(b_buf, b_buf, all_send.at[1]).wait()
        sent = s_buf.at[pl.ds(0, units - units // Z)]
        pltpu.make_async_copy(sent, sent, all_send.at[2]).wait()

    @pl.when(pipe == 1)
    def _():
        find_dest()
        pl.semaphore_wait(barrier, 2 * Z)
        for m in range(micro):
            send_halo(m)
        for m in range(micro):
            pick_rows(m, 0, 0, 0, 2 * slots)
        mask_rows(1)
        for m in range(micro):
            pass_halo(m)

        @pl.loop(0, steps)
        def _(step):
            chunk = chunk_at(step, 0)
            u = chunk // chunks
            m = u // per_micro
            await_inputs(chunk)

            @pl.when((step == 0) | (step == EARLY * half - 1))
            def _():
                @pl.loop(0, AHEAD)
                def _(other):
                    moved = other * chunks + jnp.where(step == 0, 0, half)
                    cross(moved).wait_recv()
                    settle(moved).start()

            forward(chunk).wait_recv()
            attend(chunk, 1)

            @pl.when(lax.rem(chunk, chunks) == chunks - 1)
            def _():
                picked = jnp.dot(pick[m], a_buf[u], preferred_element_type=jnp.float32)
                s_buf[u] = picked.astype(jnp.bfloat16).reshape(2, Z, CAP, CH, width)
                for other_x, turn in ((1, 2), (1, 1), (1, 3), (1, 0), (0, 2), (0, 1), (0, 3)):
                    place = x_lo if other_x == 0 else 1 - x_lo
                    spread_far(u, place * Z + lax.rem(z + turn, Z), ctx).start()
                keep_far(u).start()

        pltpu.make_async_copy(t_buf, t_buf, all_send.at[0]).wait()
        sent = s_buf.at[pl.ds(0, units - units // (2 * Z))]
        pltpu.make_async_copy(sent, sent, all_send.at[2]).wait()

    pltpu.make_async_copy(out_ref, out_ref, all_recv.at[0]).wait()

    @pl.when(ctx < ctx_count - 1)
    def _():
        for m in range(micro):
            for which in range(2):
                halo(m, which).wait_send()

    for m in range(micro):
        for which in range(2):
            if relay_z(m, which) != Z - 1:

                @pl.when(ctx == relay_z(m, which))
                def _():
                    from_relay(m, which).wait_send()


def local(queries, keys, values, doc_start, owners):
    _, micro, rows, width_q = queries.shape
    unit_width = HEAD_WIDTH
    units = micro * (width_q // unit_width)
    steps = units * (rows // CHUNK)
    bf16, f32, i32 = jnp.bfloat16, jnp.float32, jnp.int32
    dma = pltpu.SemaphoreType.DMA
    in_hbm = pl.BlockSpec(memory_space=pltpu.HBM)
    out = pl.pallas_call(
        kernel,
        out_shape=jax.ShapeDtypeStruct((micro, 2, Z, CAP, CH, width_q), bf16),
        in_specs=[in_hbm] * 5,
        out_specs=pl.BlockSpec(memory_space=pl.ANY),
        scratch_shapes=[
            pltpu.VMEM((units, rows, unit_width), bf16),
            pltpu.VMEM((DOCMAX, HEAD_WIDTH), bf16),
            pltpu.VMEM((units, rows, unit_width), bf16),
            pltpu.VMEM((AHEAD, rows, unit_width), bf16),
            pltpu.VMEM((units, rows, unit_width), bf16),
            pltpu.VMEM((units, rows, unit_width), bf16),
            pltpu.VMEM((units, 2, Z, CAP, CH, unit_width), bf16),
            pltpu.VMEM((micro, DOCMAX + rows, HEAD_WIDTH), bf16),
            pltpu.VMEM((micro, DOCMAX + rows, HEAD_WIDTH), bf16),
            pltpu.VMEM((micro, rows, SPAN), f32),
            pltpu.VMEM((micro, 2 * Z * CAP * CH, rows), bf16),
            pltpu.VMEM((2, 8, rows), i32),
            pltpu.VMEM((micro, rows), i32),
            pltpu.SMEM((micro, TRACTS_DEV), i32),
            dma((2,)),
            dma((units,)),
            dma((micro, 2)),
            dma((micro, 2)),
            dma((micro, 2)),
            dma((2,)),
            dma((2,)),
            dma((steps,)),
            dma((steps,)),
            dma((AHEAD * (rows // CHUNK),)),
            dma((3,)),
            dma((1,)),
        ],
        compiler_params=pltpu.CompilerParams(
            collective_id=0, has_side_effects=True, vmem_limit_bytes=48 * 1024 * 1024
        ),
    )(*[pltpu.with_memory_space_constraint(a, pltpu.HBM) for a in (queries, keys, values, doc_start, owners)])
    return out.reshape(1, micro, 1, 2 * Z, CAP, CH, width_q)


def solution(mesh):
    return jax.shard_map(
        local,
        mesh=mesh,
        in_specs=(
            P("pipe", None, "ctx", "tp"),
            P("pipe", None, "ctx", "tp"),
            P("pipe", None, "ctx", "tp"),
            P(None, "ctx"),
            P(None, "ctx"),
        ),
        out_specs=P("pipe", None, "ctx", None, None, None, "tp"),
        check_vma=False,
    )
```
